32 devices in a mesh: grp: 2 (over x), xfer: 16 (over z, y, core).
Axes of the slice: x: 2, y: 2, z: 4, core: 2. Of those that a mesh axis runs over, the one named last changes fastest.
Arguments:
- cq: bfloat16 [128, 2, 1536], P(('grp', 'xfer')), parts along dimension 0, may hold values from -6 to 6
- new_kv: bfloat16 [128, 2, 576], P(('grp', 'xfer')), parts along dimension 0, may hold values from -12 to 12
- cache: bfloat16 [16, 4096, 576], P('grp', 'xfer'), parts along dimension 0, may hold values from -28 to 28
- prompt_len: int32 [16], P('grp'), parts along dimension 0, may hold values from 1024 to 4096, as said below
- prefill_owner: int32 [16], P('grp'), parts along dimension 0, may hold values from 0 to 15
- cand_req: int32 [128], P('grp'), parts along dimension 0, may hold values from 0 to 7, as said below
- w_q: bfloat16 [1536, 73728], P(None, 'xfer'), may hold values from -0.15625 to 0.15625
- value_up_weight: bfloat16 [128, 512, 128], P('xfer'), may hold values from -0.25 to 0.25
- w_o: bfloat16 [16384, 7168], P('xfer'), may hold values from -0.046875 to 0.046875
Outputs:
- out: bfloat16 [128, 2, 7168], P(('grp', 'xfer')), parts along dimension 0
The draws below stay inside these ranges and needn't reach their ends.
There are 2 independent parts, one for each index of `grp`. The reference program is written for one: setup_inputs(seed, part) draws one part's arguments, and reference() takes and returns one part's arrays. A program takes and returns all parts, laid end to end along the dimension named above; an argument that names none is the same for every part. Nothing has to cross between parts.
Inputs may be any that keep to these rules, and one draw needn't show every extreme that they name: `prompt_len`: one prompt has exactly 4096 rows. `cand_req`: the 4 candidates of one device belong to one request, and devices 2k and 2k + 1 of the xfer axis hold the candidates of one request, which no other device holds.
All inputs are finite; a program needn't handle non-finite values.
Results may differ from the reference program's by a relative error of at most 0.0049.
The reference program's roundings to bfloat16 on the way count: a program that leaves them out, or rounds other values in their place, can miss the bound.
Values may be sent and summed in bfloat16 or wider, within the bound.
A program may use at most 128 MiB of HBM per device.

```python
import jax
import jax.numpy as jnp
from jax import lax

HEAD_COUNT = 128
QL = 1536
LATENT_RANK = 512
HEAD_VALUE_WIDTH = 128
D = 7168
CAND_DEV = 4
SEG = 256
STEPS = 2
KV = 576
REQS = 8
C_TOT = 64
LMAX = 4096
N_XFER = 16


def draw_cache(key, part):
    key = jax.random.fold_in(key, 7)
    drawn = jax.random.truncated_normal(key, -6.0, 6.0, (REQS, LMAX, KV), jnp.float32)
    return drawn.astype(jnp.bfloat16)


def draw_prompt_len(key, part):
    key = jax.random.fold_in(key, 3)
    length_key, pick_key = jax.random.split(key)
    lengths = jax.random.randint(length_key, (REQS,), LMAX // 4, LMAX + 1, dtype=jnp.int32)
    longest = jax.random.randint(pick_key, (), 0, REQS, dtype=jnp.int32)
    return lengths.at[longest].set(LMAX)


def draw_cand_req(key, part):
    key = jax.random.fold_in(key, 5)
    request_of_pair = jax.random.permutation(key, jnp.arange(REQS, dtype=jnp.int32))
    request_of_device = jnp.repeat(request_of_pair, 2)
    return jnp.repeat(request_of_device, CAND_DEV).astype(jnp.int32)


def place_ends(entries, rng, least, high):
    longest = entries.shape.index(max(entries.shape))
    spots = []
    for shift in (0, 1):
        where = [jax.random.randint(jax.random.fold_in(rng, axis), (), 0, length) for axis, length in enumerate(entries.shape)]
        where[longest] = (where[longest] + shift) % entries.shape[longest]
        spots.append(tuple(where))
    return entries.at[spots[0]].set(least).at[spots[1]].set(high)


def levels(own_key, dims, cuts, low, high):
    level = 1.0
    for dim, shards_of in cuts:
        steps = jax.random.uniform(jax.random.fold_in(jax.random.fold_in(own_key, 6), dim), (shards_of,), jnp.float32, low / len(cuts), high / len(cuts))
        level = level * jnp.repeat(jnp.exp(steps), dims[dim] // shards_of).reshape((-1,) + (1,) * (len(dims) - 1 - dim))
    return level


def bell_draw(stream_key, dims, spread, reach, cuts=(), kind=jnp.bfloat16):
    result = jax.random.normal(stream_key, dims, jnp.float32) * spread
    if len(cuts) > 0:
        result = levels(stream_key, dims, cuts, -0.22, 0.18) * result
    return jnp.clip(result, min=-reach, max=reach).astype(kind)


def setup_inputs(seed: int = 0, part: int = 0) -> dict:
    keys = jax.random.split(jax.random.key(seed), 10)
    part_keys = jax.random.split(jax.random.fold_in(keys[9], part), 10)
    cq = bell_draw(part_keys[0], (C_TOT, STEPS, QL), 1.0, 6.0, ((0, 16),))
    new_kv = bell_draw(part_keys[1], (C_TOT, STEPS, KV), 2.5, 12.0, ((0, 16),))
    cache = draw_cache(jax.random.fold_in(jax.random.fold_in(keys[9], part), 71), part)
    prompt_len = draw_prompt_len(jax.random.fold_in(jax.random.fold_in(keys[9], part), 71), part)
    prefill_owner = place_ends(jax.random.randint(part_keys[4], (REQS,), 0, N_XFER), jax.random.fold_in(part_keys[4], 1), 0, N_XFER - 1).astype(jnp.int32)
    cand_req = draw_cand_req(jax.random.fold_in(jax.random.fold_in(keys[9], part), 71), part)
    w_q = bell_draw(keys[6], (QL, HEAD_COUNT * KV), QL ** -0.5, 0.15625, ((1, 16),))
    value_up_weight = bell_draw(keys[7], (HEAD_COUNT, LATENT_RANK, HEAD_VALUE_WIDTH), LATENT_RANK ** -0.5, 0.25, ((0, 16),))
    w_o = bell_draw(keys[8], (HEAD_COUNT * HEAD_VALUE_WIDTH, D), (HEAD_COUNT * HEAD_VALUE_WIDTH) ** -0.5, 0.046875, ((0, 16),))
    return dict(cq=cq, new_kv=new_kv, cache=cache, prompt_len=prompt_len, prefill_owner=prefill_owner, cand_req=cand_req, w_q=w_q, value_up_weight=value_up_weight, w_o=w_o)


SCORE_SCALE = 0.135


def reference(cq, new_kv, cache, prompt_len, prefill_owner, cand_req, w_q, value_up_weight, w_o):
    projected = jnp.dot(cq.reshape(C_TOT * STEPS, QL), w_q, preferred_element_type=jnp.float32)
    queries = projected.astype(jnp.bfloat16).reshape(C_TOT, STEPS, HEAD_COUNT, KV)
    row_index = jnp.arange(LMAX, dtype=jnp.int32)
    step_index = jnp.arange(STEPS, dtype=jnp.int32)
    causal = step_index[None, :] <= step_index[:, None]
    running_peak = lax.Precision.HIGHEST

    def one_candidate(candidate):
        request = lax.dynamic_index_in_dim(cand_req, candidate, 0, keepdims=False).astype(jnp.int32)
        cached_key_rows = lax.dynamic_index_in_dim(cache, request, 0, keepdims=False).astype(jnp.float32)
        first_owner = lax.dynamic_index_in_dim(prefill_owner, request, 0, keepdims=False)
        prompt_size = lax.dynamic_index_in_dim(prompt_len, request, 0, keepdims=False)
        position = ((row_index // SEG - first_owner) % N_XFER) * SEG + row_index % SEG
        live = position < prompt_size
        query_rows = lax.dynamic_index_in_dim(queries, candidate, 0, keepdims=False).astype(jnp.float32)
        self_key_rows = lax.dynamic_index_in_dim(new_kv, candidate, 0, keepdims=False).astype(jnp.float32)
        cache_scores = jnp.einsum("shk,lk->shl", query_rows, cached_key_rows, precision=running_peak) * SCORE_SCALE
        cache_scores = jnp.where(live[None, None, :], cache_scores, -jnp.inf)
        own_scores = jnp.einsum("shk,tk->sht", query_rows, self_key_rows, precision=running_peak) * SCORE_SCALE
        own_scores = jnp.where(causal[:, None, :], own_scores, -jnp.inf)
        largest = jnp.maximum(jnp.max(cache_scores, axis=-1), jnp.max(own_scores, axis=-1))
        cache_exp = jnp.exp(cache_scores - largest[..., None])
        own_exp = jnp.exp(own_scores - largest[..., None])
        denominator = jnp.sum(cache_exp, axis=-1) + jnp.sum(own_exp, axis=-1)
        cached_prob_weights = lax.optimization_barrier((cache_exp / denominator[..., None]).astype(jnp.bfloat16))
        self_prob_weights = lax.optimization_barrier((own_exp / denominator[..., None]).astype(jnp.bfloat16))
        compressed_state = jnp.einsum("uod,de->uoe", cached_prob_weights.astype(jnp.float32), cached_key_rows[:, :LATENT_RANK], precision=running_peak)
        compressed_state = compressed_state + jnp.einsum("xgw,wi->xgi", self_prob_weights.astype(jnp.float32), self_key_rows[:, :LATENT_RANK], precision=running_peak)
        return compressed_state.astype(jnp.bfloat16)

    compressed_states = lax.map(one_candidate, jnp.arange(C_TOT, dtype=jnp.int32))
    per_head_value = jnp.einsum("diwu,wut->diwt", compressed_states.astype(jnp.float32), value_up_weight.astype(jnp.float32), precision=running_peak)
    per_head_value = per_head_value.astype(jnp.bfloat16).reshape(C_TOT * STEPS, HEAD_COUNT * HEAD_VALUE_WIDTH)
    summed = jnp.dot(per_head_value, w_o, preferred_element_type=jnp.float32)
    return summed.reshape(C_TOT, STEPS, D).astype(jnp.bfloat16)
```

```python
import functools

import jax
import jax.numpy as jnp
from jax import lax
from jax.experimental import pallas as pl
from jax.experimental.pallas import tpu as pltpu
from jax.sharding import PartitionSpec as P

SCORE_SCALE = 0.135
BF16 = jnp.bfloat16
F32 = jnp.float32
ANY = pl.BlockSpec(memory_space=pl.ANY)
VMEM = pl.BlockSpec(memory_space=pltpu.VMEM)
MIB = 1 << 20


def greet(n, me):
    barrier = pltpu.get_barrier_semaphore()

    def hello(j, carry):
        pl.semaphore_signal(
            barrier, inc=1, device_id={"xfer": lax.rem(me + j, n)},
            device_id_type=pl.DeviceIdType.MESH,
        )
        return carry

    lax.fori_loop(1, n, hello, 0)
    pl.semaphore_wait(barrier, n - 1)


def remote(src, dst, send, recv, device):
    return pltpu.make_async_remote_copy(
        src_ref=src, dst_ref=dst, send_sem=send, recv_sem=recv,
        device_id={"xfer": device}, device_id_type=pl.DeviceIdType.MESH,
    )


def loop(low, high, body):
    def step(i, carry):
        body(i)
        return carry

    lax.fori_loop(low, high, step, 0)


def exchange_kernel(
    n, cq_ref, wq_ref, out_ref, q_ref, k_ref,
    cq_all, wq_v, qs, wq_sem, cq_send, cq_recv, q_send, q_recv,
    k_send, k_recv, f_send, f_recv, local_sem,
):
    me = lax.axis_index("xfer")
    chips = n // 2
    chip = me // 2
    core = lax.rem(me, 2)
    sibling = chip * 2 + 1 - core
    pairs = wq_v.shape[0]
    width = wq_v.shape[2]
    kv = width // 2
    rows = cq_ref.shape[0]

    def load_wq(p):
        return pltpu.make_async_copy(
            wq_ref.at[:, pl.ds(pl.multiple_of(p * width, 128), width)], wq_v.at[p], wq_sem.at[p]
        )

    loop(0, pairs, lambda p: load_wq(p).start())
    own_block = pltpu.make_async_copy(out_ref.at[chip], k_ref.at[me], local_sem.at[0])
    own_block.start()
    greet(n, me)

    def cq_copy(j):
        return remote(
            cq_ref, cq_all.at[me], cq_send.at[j], cq_recv.at[me], lax.rem(me + j, n)
        )

    loop(1, n, lambda j: cq_copy(j).start())
    cq_all[me] = cq_ref[...]

    def block_copy(j, half):
        target = lax.rem(chip + j, chips)
        return remote(
            out_ref.at[target, half], k_ref.at[me, half],
            k_send.at[j, half], k_recv.at[me], target * 2 + half,
        )

    def send_blocks(j):
        block_copy(j, 0).start()
        block_copy(j, 1).start()

    sibling_copy = remote(
        out_ref.at[chip], k_ref.at[me], k_send.at[0, 0], k_recv.at[me], sibling
    )
    sibling_copy.start()
    loop(1, chips, send_blocks)

    def wait_cq(j):
        s = lax.rem(me + n - j, n)
        remote(cq_ref, cq_all.at[s], cq_send.at[j], cq_recv.at[s], s).wait_recv()

    loop(1, n, wait_cq)
    x = cq_all[...].reshape(n * rows, cq_ref.shape[1]).astype(BF16)

    def project(p):
        load_wq(p).wait()
        y = jnp.dot(x, wq_v[p], preferred_element_type=F32)
        first = y[:, :kv].reshape(n, rows, kv)
        second = y[:, kv:].reshape(n, rows, kv)
        qs[:, pl.ds(pl.multiple_of(p * 2 * rows, 16), 2 * rows), :] = jnp.concatenate(
            [first, second], axis=1
        ).astype(BF16)

    loop(0, pairs, project)

    def q_copy(j):
        d = lax.rem(me + j, n)
        return remote(qs.at[d], q_ref.at[me], q_send.at[j], q_recv.at[me], d)

    loop(1, n, lambda j: q_copy(j).start())
    own_q = pltpu.make_async_copy(qs.at[me], q_ref.at[me], local_sem.at[1])
    own_q.start()

    def forward_copy(s):
        return remote(k_ref.at[s, core], k_ref.at[s, core], f_send.at[s], f_recv.at[s], sibling)

    def source(j, other):
        return lax.rem(chip + chips - j, chips) * 2 + other

    def relay(j):
        for other in (0, 1):
            s = source(j, other)
            remote(
                out_ref.at[0, 0], k_ref.at[s, core], k_send.at[0, 0], k_recv.at[s], s
            ).wait_recv()
            forward_copy(s).start()

    loop(1, chips, relay)

    def finish(j):
        for other in (0, 1):
            s = source(j, other)
            remote(
                k_ref.at[s, 1 - core], k_ref.at[s, 1 - core], f_send.at[s], f_recv.at[s], sibling
            ).wait_recv()
            forward_copy(s).wait_send()
        block_copy(j, 0).wait_send()
        block_copy(j, 1).wait_send()

    loop(1, chips, finish)
    sibling_copy.wait_send()
    remote(
        out_ref.at[chip], k_ref.at[sibling], k_send.at[0, 0], k_recv.at[sibling], sibling
    ).wait_recv()

    def finish_q(j):
        s = lax.rem(me + n - j, n)
        remote(qs.at[me], q_ref.at[s], q_send.at[j], q_recv.at[s], s).wait_recv()
        q_copy(j).wait_send()
        cq_copy(j).wait_send()

    loop(1, n, finish_q)
    own_q.wait()
    own_block.wait()


def attend_kernel(
    n, key_chunk, q_ref, k_ref, live_ref, own_key_ref, own_bias_ref, lat_ref,
    lat_out, score, total, l_send, l_recv, local_sem,
):
    me = lax.axis_index("xfer")
    per_source = q_ref.shape[1]
    kv = q_ref.shape[2]
    latent = lat_ref.shape[2]
    block = score.shape[0]
    keys = k_ref.shape[0]
    group = block // per_source
    blocks = n // group
    chunks = keys // key_chunk
    own_width = own_key_ref.shape[0]
    nt = (((1,), (1,)), ((), ()))
    greet(n, me)

    def lat_copy(d):
        return remote(lat_out.at[d], lat_ref.at[me], l_send.at[d], l_recv.at[me], d)

    def own_copy():
        return pltpu.make_async_copy(lat_out.at[me], lat_ref.at[me], local_sem)

    def each_block(b):
        first = lax.rem(me // group + 1 + b, blocks) * group
        q = q_ref[pl.ds(first, group)].reshape(block, kv)
        own = (
            lax.dot_general(q, own_key_ref[...], nt, preferred_element_type=F32) * SCORE_SCALE
            + own_bias_ref[...]
        )

        def scores(c, top):
            at = pl.ds(pl.multiple_of(c * key_chunk, key_chunk), key_chunk)
            s = (
                lax.dot_general(q, k_ref[at, :], nt, preferred_element_type=F32) * SCORE_SCALE
                + live_ref[:, at]
            )
            score[:, at] = s
            for i in range(0, key_chunk, 128):
                top = jnp.maximum(top, s[:, i : i + 128])
            return top

        top = lax.fori_loop(0, chunks, scores, own)
        top = jnp.max(top, axis=1, keepdims=True)
        own = jnp.exp(own - top)

        def sums(c, acc):
            at = pl.ds(pl.multiple_of(c * key_chunk, key_chunk), key_chunk)
            e = jnp.exp(score[:, at] - top)
            score[:, at] = e
            for i in range(0, key_chunk, 128):
                acc = acc + e[:, i : i + 128]
            return acc

        acc = lax.fori_loop(0, chunks, sums, own)
        inverse = 1.0 / jnp.sum(acc, axis=1, keepdims=True)
        total[...] = jnp.dot(
            (own * inverse).astype(BF16), own_key_ref[:, :latent], preferred_element_type=F32
        )

        def gather(c):
            at = pl.ds(pl.multiple_of(c * key_chunk, key_chunk), key_chunk)
            total[...] += jnp.dot(
                (score[:, at] * inverse).astype(BF16), k_ref[at, :latent],
                preferred_element_type=F32,
            )

        loop(0, chunks, gather)
        lat_out[pl.ds(first, group)] = total[...].astype(BF16).reshape(group, per_source, latent)

        def send(i):
            d = first + i

            @pl.when(d != me)
            def _():
                lat_copy(d).start()

            @pl.when(d == me)
            def _():
                own_copy().start()

        loop(0, group, send)

    loop(0, blocks, each_block)

    def finish(j):
        s = lax.rem(me + j, n)
        remote(lat_out.at[me], lat_ref.at[s], l_send.at[s], l_recv.at[s], s).wait_recv()
        lat_copy(s).wait_send()

    loop(1, n, finish)
    own_copy().wait()


def output_kernel(
    n, lat_ref, up_ref, wo_ref, o_ref,
    hv, wo_v, part, x_in, snd, rcv, wo_sem, x_send, x_recv, s_send, s_recv,
):
    me = lax.axis_index("xfer")
    chips = n // 2
    chip = me // 2
    core = lax.rem(me, 2)
    sibling = chip * 2 + 1 - core
    chunks = wo_v.shape[0]
    cw = wo_v.shape[3]
    half = chunks * cw
    heads, latent, value = up_ref.shape
    rows = lat_ref.shape[1] // heads

    def load_wo(j, side):
        return pltpu.make_async_copy(
            wo_ref.at[:, pl.ds(pl.multiple_of(j * cw + side * half, 128), cw)],
            wo_v.at[j, side], wo_sem.at[j, side],
        )

    def load(j):
        load_wo(j, 0).start()
        load_wo(j, 1).start()

    loop(0, chunks, load)
    greet(n, me)
    for p in range(heads // 2):
        z = lat_ref[:, p * 2 * rows : (p + 1) * 2 * rows, :].astype(F32)
        for i in (0, 1):
            h = 2 * p + i
            z_head = z[:, i * rows : (i + 1) * rows, :].reshape(n * rows, latent).astype(BF16)
            y = jnp.dot(z_head, up_ref[h], preferred_element_type=F32)
            y = y.reshape(chips, 2, rows, value)
            hv[0 : chips * rows, h * value : (h + 1) * value] = (
                y[:, 0].reshape(chips * rows, value).astype(BF16)
            )
            hv[chips * rows :, h * value : (h + 1) * value] = (
                y[:, 1].reshape(chips * rows, value).astype(BF16)
            )

    def core_copy(j):
        return remote(part.at[j, 1 - core], x_in.at[j], x_send.at[j], x_recv.at[j], sibling)

    def multiply(j):
        for side in (0, 1):
            load_wo(j, side).wait()
            y = jnp.dot(hv[...], wo_v[j, side], preferred_element_type=F32)
            part[j, 0, side] = y[: chips * rows]
            part[j, 1, side] = y[chips * rows :]
        core_copy(j).start()

    def chip_copy(j, i):
        t = lax.rem(chip + i, chips)
        return remote(
            snd.at[j, t], rcv.at[j, chip], s_send.at[j, i], s_recv.at[j, chip], t * 2 + core
        )

    def combine(j):
        core_copy(j).wait_recv()
        both = part[j, core] + x_in[j]
        packed = jnp.concatenate(
            [both[0].reshape(chips, rows, cw), both[1].reshape(chips, rows, cw)], axis=1
        )
        snd[j] = packed.astype(BF16)
        loop(1, chips, lambda i: chip_copy(j, i).start())

    multiply(0)

    def step(j):
        multiply(j)
        combine(j - 1)

    loop(1, chunks, step)
    combine(chunks - 1)

    def finish(j):
        def wait(i):
            s = lax.rem(chip + chips - i, chips)
            remote(
                snd.at[j, 0], rcv.at[j, s], s_send.at[j, i], s_recv.at[j, s], s * 2 + core
            ).wait_recv()
            chip_copy(j, i).wait_send()

        loop(1, chips, wait)
        core_copy(j).wait_send()
        rcv[j, chip] = snd[j, chip]
        y = jnp.sum(rcv[j].astype(F32), axis=0)
        o_ref[:, pl.ds(pl.multiple_of(j * cw, 128), cw)] = y[:rows].astype(BF16)
        o_ref[:, pl.ds(pl.multiple_of(half + j * cw, 128), cw)] = y[rows:].astype(BF16)

    loop(0, chunks, finish)


def params(collective_id, mib):
    return pltpu.CompilerParams(
        collective_id=collective_id, has_side_effects=True, vmem_limit_bytes=mib * MIB
    )


def shards(cq, new_kv, cache, prompt_len, prefill_owner, cand_req, w_q, value_up_weight, w_o):
    n = lax.axis_size("xfer")
    device = lax.axis_index("xfer")
    cand, steps, q_width = cq.shape
    heads, latent, value = value_up_weight.shape
    segment, kv = cache.shape[1:]
    length = segment * n
    rows = cand * steps
    model = w_o.shape[1]
    per_source = heads * rows
    chips = n // 2
    dma = pltpu.SemaphoreType.DMA

    request_of_chip = cand_req.reshape(chips, 2 * cand)[:, 0]
    outgoing = jnp.take(cache, request_of_chip, axis=0, mode="clip").reshape(
        chips, 2, segment // 2, kv
    )
    my_request = lax.dynamic_index_in_dim(request_of_chip, device // 2, 0, keepdims=False)
    my_length = lax.dynamic_index_in_dim(prompt_len, my_request, 0, keepdims=False)
    first_owner = lax.dynamic_index_in_dim(prefill_owner, my_request, 0, keepdims=False)
    row_index = jnp.arange(length, dtype=jnp.int32)
    position = (row_index // segment - first_owner) % n * segment + row_index % segment
    live = jnp.where(position < my_length, 0.0, -jnp.inf).astype(F32)[None, :]

    pairs = heads // 2
    queries, keys = pl.pallas_call(
        functools.partial(exchange_kernel, n),
        out_shape=(
            jax.ShapeDtypeStruct((n, per_source, kv), BF16),
            jax.ShapeDtypeStruct((n, 2, segment // 2, kv), BF16),
        ),
        in_specs=[VMEM, ANY, ANY],
        out_specs=(ANY, ANY),
        scratch_shapes=[
            pltpu.VMEM((n, rows, q_width), F32),
            pltpu.VMEM((pairs, q_width, 2 * kv), BF16),
            pltpu.VMEM((n, per_source, kv), BF16),
            dma((pairs,)),
            dma((n,)), dma((n,)), dma((n,)), dma((n,)),
            dma((chips, 2)), dma((n,)), dma((n,)), dma((n,)),
            dma((2,)),
        ],
        compiler_params=params(0, 40),
        name="exchange",
    )(cq.reshape(rows, q_width).astype(F32), w_q, outgoing)

    block = 256
    own_keys = jnp.zeros((128, kv), BF16).at[:rows].set(new_kv.reshape(rows, kv))
    row = jnp.arange(block, dtype=jnp.int32)[:, None] % rows
    col = jnp.arange(128, dtype=jnp.int32)[None, :]
    seen = (col // steps == row // steps) & (col % steps <= row % steps)
    own_bias = jnp.where(seen, 0.0, -jnp.inf).astype(F32)
    latents = pl.pallas_call(
        functools.partial(attend_kernel, n, 512),
        out_shape=jax.ShapeDtypeStruct((n, per_source, latent), BF16),
        in_specs=[VMEM] * 5,
        out_specs=ANY,
        scratch_shapes=[
            pltpu.VMEM((n, per_source, latent), BF16),
            pltpu.VMEM((block, length), F32),
            pltpu.VMEM((block, latent), F32),
            dma((n,)), dma((n,)), dma,
        ],
        compiler_params=params(1, 48),
        name="attend",
    )(queries, keys.reshape(length, kv), live, own_keys, own_bias)

    cw = 512
    chunks = model // (2 * cw)
    out = pl.pallas_call(
        functools.partial(output_kernel, n),
        out_shape=jax.ShapeDtypeStruct((rows, model), BF16),
        in_specs=[VMEM, VMEM, ANY],
        out_specs=VMEM,
        scratch_shapes=[
            pltpu.VMEM((n * rows, heads * value), BF16),
            pltpu.VMEM((chunks, 2, heads * value, cw), BF16),
            pltpu.VMEM((chunks, 2, 2, chips * rows, cw), F32),
            pltpu.VMEM((chunks, 2, chips * rows, cw), F32),
            pltpu.VMEM((chunks, chips, 2 * rows, cw), BF16),
            pltpu.VMEM((chunks, chips, 2 * rows, cw), BF16),
            dma((chunks, 2)), dma((chunks,)), dma((chunks,)),
            dma((chunks, chips)), dma((chunks, chips)),
        ],
        compiler_params=params(2, 44),
        name="output",
    )(latents, value_up_weight, w_o)
    return out.reshape(cand, steps, model)


def solution(mesh):
    in_specs = (
        P(("grp", "xfer"), None, None),
        P(("grp", "xfer"), None, None),
        P("grp", "xfer", None),
        P("grp"),
        P("grp"),
        P("grp"),
        P(None, "xfer"),
        P("xfer", None, None),
        P("xfer", None),
    )
    out_specs = P(("grp", "xfer"), None, None)
    return jax.shard_map(shards, mesh=mesh, in_specs=in_specs, out_specs=out_specs, check_vma=False)
```

```python
import functools

import jax
import jax.numpy as jnp
from jax import lax
from jax.experimental import pallas as pl
from jax.experimental.pallas import tpu as pltpu
from jax.sharding import PartitionSpec as P

SCORE_SCALE = 0.135
BF16 = jnp.bfloat16
F32 = jnp.float32
ANY = pl.BlockSpec(memory_space=pl.ANY)
VMEM = pl.BlockSpec(memory_space=pltpu.VMEM)
MIB = 1 << 20


def greet(n, me):
    barrier = pltpu.get_barrier_semaphore()

    def hello(j, carry):
        pl.semaphore_signal(
            barrier, inc=1, device_id={"xfer": me ^ j},
            device_id_type=pl.DeviceIdType.MESH,
        )
        return carry

    lax.fori_loop(1, n, hello, 0)
    pl.semaphore_wait(barrier, n - 1)


def remote(src, dst, send, recv, device):
    return pltpu.make_async_remote_copy(
        src_ref=src, dst_ref=dst, send_sem=send, recv_sem=recv,
        device_id={"xfer": device}, device_id_type=pl.DeviceIdType.MESH,
    )


def loop(low, high, body):
    def step(i, carry):
        body(i)
        return carry

    lax.fori_loop(low, high, step, 0)


def prepare_kernel(cand, request_ref, length_ref, owner_ref, cache_ref, own_ref,
                   out_ref, live_ref, own_key_ref, sems):
    chips, _, width = live_ref.shape
    segment = width // 2

    def pick(t):
        return pltpu.make_async_copy(
            cache_ref.at[request_ref[t * 2 * cand]], out_ref.at[t], sems.at[t]
        )

    loop(0, chips, lambda t: pick(t).start())
    request = request_ref[lax.axis_index("xfer") // 2 * 2 * cand]
    chip = lax.broadcasted_iota(jnp.int32, live_ref.shape, 0)
    col = lax.broadcasted_iota(jnp.int32, live_ref.shape, 2)
    odd = (col >= segment).astype(jnp.int32)
    order = chip * 2 + odd - owner_ref[request]
    order = jnp.where(order < 0, order + 2 * chips, order)
    position = order * segment + col - odd * segment
    live_ref[...] = jnp.where(position < length_ref[request], 0.0, -jnp.inf).astype(F32)
    own_key_ref[...] = jnp.zeros_like(own_key_ref)
    own_key_ref[: own_ref.shape[0]] = own_ref[...]
    loop(0, chips, lambda t: pick(t).wait())


def attend_kernel(
    n, steps, early, cq_ref, wq_ref, out_ref, live_ref, own_key_ref, lat_ref,
    cq_all, wq_v, qs, q_in, k_in, lat_out, score, own_score, top_ref, sum_ref, total,
    wq_sem, cq_send, cq_recv, q_send, q_recv, k_send, k_recv, f_send, f_recv,
    l_send, l_recv, local_sem,
):
    me = lax.axis_index("xfer")
    chips = n // 2
    chip = me // 2
    core = lax.rem(me, 2)
    sibling = me ^ 1
    pairs, _, width = wq_v.shape
    kv = width // 2
    rows = cq_ref.shape[0]
    per_source, latent = lat_out.shape[1:]
    pair_keys = live_ref.shape[2]
    block = total.shape[0]
    group = block // per_source
    blocks = n // group
    nt = (((1,), (1,)), ((), ()))

    def load_wq(p):
        return pltpu.make_async_copy(
            wq_ref.at[:, pl.ds(pl.multiple_of(p * width, 128), width)], wq_v.at[p], wq_sem.at[p]
        )

    loop(0, pairs, lambda p: load_wq(p).start())
    own_block = pltpu.make_async_copy(out_ref.at[chip], k_in.at[me], local_sem.at[0])
    own_block.start()
    greet(n, me)

    def cq_copy(j):
        return remote(cq_ref, cq_all.at[me], cq_send.at[j], cq_recv.at[me], me ^ j)

    loop(1, n, lambda j: cq_copy(j).start())
    cq_all[me] = cq_ref[...]

    def block_copy(j, half):
        t = chip ^ j
        return remote(
            out_ref.at[t, half], k_in.at[me, half], k_send.at[j, half], k_recv.at[me], t * 2 + half
        )

    def send_blocks(r):
        block_copy(chips - r, 0).start()
        block_copy(chips - r, 1).start()

    sibling_copy = remote(
        out_ref.at[chip], k_in.at[me], k_send.at[0, 0], k_recv.at[me], sibling
    )
    loop(1, early, send_blocks)

    def wait_cq(j):
        s = me ^ j
        remote(cq_ref, cq_all.at[s], cq_send.at[j], cq_recv.at[s], s).wait_recv()

    loop(1, n, wait_cq)
    x = cq_all[...].reshape(n * rows, cq_ref.shape[1]).astype(BF16)

    def project(p):
        load_wq(p).wait()
        y = jnp.dot(x, wq_v[p], preferred_element_type=F32)
        first = y[:, :kv].reshape(n, rows, kv)
        second = y[:, kv:].reshape(n, rows, kv)
        qs[:, pl.ds(pl.multiple_of(p * 2 * rows, 16), 2 * rows), :] = jnp.concatenate(
            [first, second], axis=1
        ).astype(BF16)

    loop(0, pairs, project)

    def q_copy(j):
        return remote(qs.at[me ^ j], q_in.at[me], q_send.at[j], q_recv.at[me], me ^ j)

    loop(1, n, lambda r: q_copy(n - r).start())
    sibling_copy.start()
    loop(early, chips, send_blocks)
    q_in[me] = qs[me]

    row = lax.rem(lax.broadcasted_iota(jnp.int32, (block, 128), 0), rows)
    col = lax.broadcasted_iota(jnp.int32, (block, 128), 1)
    behind = row - col
    seen = (behind >= 0) & (behind <= lax.rem(row, steps))
    own_bias = jnp.where(seen, 0.0, -jnp.inf).astype(F32)

    def wait_q(r):
        s = me ^ (n - r)
        remote(qs.at[me], q_in.at[s], q_send.at[n - r], q_recv.at[s], s).wait_recv()

    loop(1, n, wait_q)

    def queries(b):
        return q_in[pl.ds(b * group, group)].reshape(block, kv)

    def own_terms(b):
        s = (
            lax.dot_general(queries(b), own_key_ref[...], nt, preferred_element_type=F32)
            * SCORE_SCALE
            + own_bias
        )
        own_score[b] = s
        top = jnp.maximum(s, -1e30)
        top_ref[b] = top
        sum_ref[b] = jnp.exp(s - top)

    loop(0, blocks, own_terms)

    def pair_scores(t):
        keys = k_in[pl.ds(2 * t, 2)].reshape(pair_keys, kv)
        live = live_ref[t]

        def block_scores(b):
            s = (
                lax.dot_general(queries(b), keys, nt, preferred_element_type=F32) * SCORE_SCALE
                + live
            )
            score[b, t] = s
            old = top_ref[b]
            top = old
            for i in range(0, pair_keys, 128):
                top = jnp.maximum(top, s[:, i : i + 128])
            acc = sum_ref[b] * jnp.exp(old - top)
            for i in range(0, pair_keys, 128):
                acc = acc + jnp.exp(s[:, i : i + 128] - top)
            top_ref[b] = top
            sum_ref[b] = acc

        loop(0, blocks, block_scores)

    def forward_copy(s):
        return remote(k_in.at[s, core], k_in.at[s, core], f_send.at[s], f_recv.at[s], sibling)

    def relay(t):
        for other in (0, 1):
            s = t * 2 + other
            remote(
                out_ref.at[0, 0], k_in.at[s, core], k_send.at[0, 0], k_recv.at[s], s
            ).wait_recv()
            forward_copy(s).start()

    def arrive(t):
        for other in (0, 1):
            s = t * 2 + other
            remote(
                k_in.at[s, 1 - core], k_in.at[s, 1 - core], f_send.at[s], f_recv.at[s], sibling
            ).wait_recv()

    relay(chip ^ (chips - 1))

    def receive(r):
        relay(chip ^ (chips - r))
        t = chip ^ (chips - r + 1)
        arrive(t)
        pair_scores(t)

    loop(2, chips, receive)
    own_block.wait()
    remote(
        out_ref.at[chip], k_in.at[sibling], k_send.at[0, 0], k_recv.at[sibling], sibling
    ).wait_recv()
    pair_scores(chip)
    arrive(chip ^ 1)
    pair_scores(chip ^ 1)

    def lat_copy(d):
        return remote(lat_out.at[d], lat_ref.at[me], l_send.at[d], l_recv.at[me], d)

    def own_copy():
        return pltpu.make_async_copy(lat_out.at[me], lat_ref.at[me], local_sem.at[1])

    def each_block(r):
        b = (me // group) ^ (blocks - 1 - r)
        lane_top = top_ref[b]
        top = jnp.max(lane_top, axis=1, keepdims=True)
        inverse = 1.0 / jnp.sum(sum_ref[b] * jnp.exp(lane_top - top), axis=1, keepdims=True)
        total[...] = jnp.dot(
            (jnp.exp(own_score[b] - top) * inverse).astype(BF16), own_key_ref[:, :latent],
            preferred_element_type=F32,
        )

        def gather(t):
            weights = (jnp.exp(score[b, t] - top) * inverse).astype(BF16)
            values = k_in[pl.ds(2 * t, 2)].reshape(pair_keys, kv)[:, :latent]
            total[...] += jnp.dot(weights, values, preferred_element_type=F32)

        loop(0, chips, gather)
        first = b * group
        lat_out[pl.ds(first, group)] = total[...].astype(BF16).reshape(group, per_source, latent)

        def send(i):
            d = first + i

            @pl.when(d != me)
            def _():
                lat_copy(d).start()

            @pl.when(d == me)
            def _():
                own_copy().start()

        loop(0, group, send)

    loop(0, blocks, each_block)

    def finish(j):
        s = me ^ j
        q_copy(j).wait_send()
        cq_copy(j).wait_send()
        remote(lat_out.at[me], lat_ref.at[s], l_send.at[s], l_recv.at[s], s).wait_recv()
        lat_copy(s).wait_send()

    def finish_blocks(j):
        for half in (0, 1):
            block_copy(j, half).wait_send()
            forward_copy((chip ^ j) * 2 + half).wait_send()

    sibling_copy.wait_send()
    loop(1, chips, finish_blocks)
    loop(1, n, finish)
    own_copy().wait()


def output_kernel(
    n, lat_ref, up_ref, wo_ref, o_ref,
    hv, wo_v, part, x_in, snd, rcv, wo_sem, x_send, x_recv, s_send, s_recv,
):
    me = lax.axis_index("xfer")
    chips = n // 2
    chip = me // 2
    core = lax.rem(me, 2)
    sibling = chip * 2 + 1 - core
    chunks = wo_v.shape[0]
    cw = wo_v.shape[3]
    half = chunks * cw
    heads, latent, value = up_ref.shape
    rows = lat_ref.shape[1] // heads

    def load_wo(j, side):
        return pltpu.make_async_copy(
            wo_ref.at[:, pl.ds(pl.multiple_of(j * cw + side * half, 128), cw)],
            wo_v.at[j, side], wo_sem.at[j, side],
        )

    def load(j):
        load_wo(j, 0).start()
        load_wo(j, 1).start()

    loop(0, chunks, load)
    greet(n, me)
    for p in range(heads // 2):
        z = lat_ref[:, p * 2 * rows : (p + 1) * 2 * rows, :].astype(F32)
        for i in (0, 1):
            h = 2 * p + i
            z_head = z[:, i * rows : (i + 1) * rows, :].reshape(n * rows, latent).astype(BF16)
            y = jnp.dot(z_head, up_ref[h], preferred_element_type=F32)
            y = y.reshape(chips, 2, rows, value)
            hv[0 : chips * rows, h * value : (h + 1) * value] = (
                y[:, 0].reshape(chips * rows, value).astype(BF16)
            )
            hv[chips * rows :, h * value : (h + 1) * value] = (
                y[:, 1].reshape(chips * rows, value).astype(BF16)
            )

    def core_copy(j):
        return remote(part.at[j, 1 - core], x_in.at[j], x_send.at[j], x_recv.at[j], sibling)

    def multiply(j):
        for side in (0, 1):
            load_wo(j, side).wait()
            y = jnp.dot(hv[...], wo_v[j, side], preferred_element_type=F32)
            part[j, 0, side] = y[: chips * rows]
            part[j, 1, side] = y[chips * rows :]
        core_copy(j).start()

    def chip_copy(j, i):
        t = chip ^ i
        return remote(
            snd.at[j, t], rcv.at[j, chip], s_send.at[j, i], s_recv.at[j, chip], t * 2 + core
        )

    def combine(j):
        core_copy(j).wait_recv()
        both = part[j, core] + x_in[j]
        packed = jnp.concatenate(
            [both[0].reshape(chips, rows, cw), both[1].reshape(chips, rows, cw)], axis=1
        )
        snd[j] = packed.astype(BF16)
        loop(1, chips, lambda i: chip_copy(j, chips - i).start())

    multiply(0)

    def step(j):
        multiply(j)
        combine(j - 1)

    loop(1, chunks, step)
    combine(chunks - 1)

    def finish(j):
        def wait(i):
            s = chip ^ i
            remote(
                snd.at[j, 0], rcv.at[j, s], s_send.at[j, i], s_recv.at[j, s], s * 2 + core
            ).wait_recv()
            chip_copy(j, i).wait_send()

        loop(1, chips, wait)
        core_copy(j).wait_send()
        rcv[j, chip] = snd[j, chip]
        y = jnp.sum(rcv[j].astype(F32), axis=0)
        o_ref[:, pl.ds(pl.multiple_of(j * cw, 128), cw)] = y[:rows].astype(BF16)
        o_ref[:, pl.ds(pl.multiple_of(half + j * cw, 128), cw)] = y[rows:].astype(BF16)

    loop(0, chunks, finish)


def params(collective_id, mib):
    return pltpu.CompilerParams(
        collective_id=collective_id, has_side_effects=True, vmem_limit_bytes=mib * MIB
    )


def shards(cq, new_kv, cache, prompt_len, prefill_owner, cand_req, w_q, value_up_weight, w_o):
    n = lax.axis_size("xfer")
    cand, steps, q_width = cq.shape
    heads, latent, value = value_up_weight.shape
    segment, kv = cache.shape[1:]
    rows = cand * steps
    model = w_o.shape[1]
    per_source = heads * rows
    chips = n // 2
    dma = pltpu.SemaphoreType.DMA

    smem = pl.BlockSpec(memory_space=pltpu.SMEM)
    outgoing, live, own_keys = pl.pallas_call(
        functools.partial(prepare_kernel, cand),
        out_shape=(
            jax.ShapeDtypeStruct((chips, segment, kv), BF16),
            jax.ShapeDtypeStruct((chips, 1, 2 * segment), F32),
            jax.ShapeDtypeStruct((128, kv), BF16),
        ),
        in_specs=[smem, smem, smem, ANY, VMEM],
        out_specs=(ANY, VMEM, VMEM),
        scratch_shapes=[dma((chips,))],
        name="prepare",
    )(cand_req, prompt_len, prefill_owner, cache, new_kv.reshape(rows, kv))

    pairs = heads // 2
    block = 256
    blocks = n * per_source // block
    latents = pl.pallas_call(
        functools.partial(attend_kernel, n, steps, chips // 4 + 1),
        out_shape=jax.ShapeDtypeStruct((n, per_source, latent), BF16),
        in_specs=[VMEM, ANY, ANY, VMEM, VMEM],
        out_specs=ANY,
        scratch_shapes=[
            pltpu.VMEM((n, rows, q_width), F32),
            pltpu.VMEM((pairs, q_width, 2 * kv), BF16),
            pltpu.VMEM((n, per_source, kv), BF16),
            pltpu.VMEM((n, per_source, kv), BF16),
            pltpu.VMEM((n, 2, segment // 2, kv), BF16),
            pltpu.VMEM((n, per_source, latent), BF16),
            pltpu.VMEM((blocks, chips, block, 2 * segment), F32),
            pltpu.VMEM((blocks, block, 128), F32),
            pltpu.VMEM((blocks, block, 128), F32),
            pltpu.VMEM((blocks, block, 128), F32),
            pltpu.VMEM((block, latent), F32),
            dma((pairs,)),
            dma((n,)), dma((n,)), dma((n,)), dma((n,)),
            dma((chips, 2)), dma((n,)), dma((n,)), dma((n,)),
            dma((n,)), dma((n,)), dma((2,)),
        ],
        compiler_params=params(0, 60),
        name="attend",
    )(
        cq.reshape(rows, q_width).astype(F32), w_q,
        outgoing.reshape(chips, 2, segment // 2, kv), live, own_keys,
    )

    cw = 512
    chunks = model // (2 * cw)
    out = pl.pallas_call(
        functools.partial(output_kernel, n),
        out_shape=jax.ShapeDtypeStruct((rows, model), BF16),
        in_specs=[VMEM, VMEM, ANY],
        out_specs=VMEM,
        scratch_shapes=[
            pltpu.VMEM((n * rows, heads * value), BF16),
            pltpu.VMEM((chunks, 2, heads * value, cw), BF16),
            pltpu.VMEM((chunks, 2, 2, chips * rows, cw), F32),
            pltpu.VMEM((chunks, 2, chips * rows, cw), F32),
            pltpu.VMEM((chunks, chips, 2 * rows, cw), BF16),
            pltpu.VMEM((chunks, chips, 2 * rows, cw), BF16),
            dma((chunks, 2)), dma((chunks,)), dma((chunks,)),
            dma((chunks, chips)), dma((chunks, chips)),
        ],
        compiler_params=params(1, 44),
        name="output",
    )(latents, value_up_weight, w_o)
    return out.reshape(cand, steps, model)


def solution(mesh):
    in_specs = (
        P(("grp", "xfer"), None, None),
        P(("grp", "xfer"), None, None),
        P("grp", "xfer", None),
        P("grp"),
        P("grp"),
        P("grp"),
        P(None, "xfer"),
        P("xfer", None, None),
        P("xfer", None),
    )
    out_specs = P(("grp", "xfer"), None, None)
    return jax.shard_map(shards, mesh=mesh, in_specs=in_specs, out_specs=out_specs, check_vma=False)
```

```python
import functools

import jax
import jax.numpy as jnp
from jax import lax
from jax.experimental import pallas as pl
from jax.experimental.pallas import tpu as pltpu
from jax.sharding import PartitionSpec as P

SCORE_SCALE = 0.135
BF16 = jnp.bfloat16
F32 = jnp.float32
ANY = pl.BlockSpec(memory_space=pl.ANY)
VMEM = pl.BlockSpec(memory_space=pltpu.VMEM)
MIB = 1 << 20


def greet(n, me):
    barrier = pltpu.get_barrier_semaphore()

    def hello(j, carry):
        pl.semaphore_signal(
            barrier, inc=1, device_id={"xfer": me ^ j},
            device_id_type=pl.DeviceIdType.MESH,
        )
        return carry

    lax.fori_loop(1, n, hello, 0)
    pl.semaphore_wait(barrier, n - 1)


def remote(src, dst, send, recv, device):
    return pltpu.make_async_remote_copy(
        src_ref=src, dst_ref=dst, send_sem=send, recv_sem=recv,
        device_id={"xfer": device}, device_id_type=pl.DeviceIdType.MESH,
    )


def loop(low, high, body):
    def step(i, carry):
        body(i)
        return carry

    lax.fori_loop(low, high, step, 0)


def attend_kernel(
    n, cand, steps, early, request_ref, length_ref, owner_ref, cq_ref, wq_ref, cache_ref,
    own_key_ref, lat_ref,
    cq_all, qs, q_in, out_ref, k_in, v_in, lat_out, own_score, top_ref, sum_ref, total,
    wq_sem, cq_send, cq_recv, q_send, q_recv, k_send, k_recv, f_send, f_recv,
    l_send, l_recv, c_send, c_recv, local_sem,
):
    me = lax.axis_index("xfer")
    chips = n // 2
    chip = me // 2
    core = lax.rem(me, 2)
    sibling = me ^ 1
    kv = q_in.shape[2]
    width = 2 * kv
    pairs = wq_ref.shape[1] // width
    rows = cq_ref.shape[0] // 2
    per_source, latent = lat_out.shape[1:]
    half_keys = k_in.shape[3]
    segment = 2 * half_keys
    pair_keys = 2 * segment
    block = total.shape[0]
    group = block // per_source
    blocks = n // group
    nt = (((1,), (1,)), ((), ()))

    def cq_copy(j):
        return remote(cq_ref, cq_all.at[me], cq_send.at[j], cq_recv.at[me], me ^ (2 * j))

    def cq_forward(s):
        return remote(cq_all.at[s], cq_all.at[s], c_send.at[s], c_recv.at[s], sibling)

    def block_copy(j, half):
        t = chip ^ j
        return remote(
            out_ref.at[t, half], k_in.at[me, half], k_send.at[j, half], k_recv.at[me], t * 2 + half
        )

    def send_blocks(r):
        block_copy(chips - r, 0).start()
        block_copy(chips - r, 1).start()

    sibling_copy = remote(
        out_ref.at[chip], k_in.at[me], k_send.at[0, 0], k_recv.at[me], sibling
    )

    def start_phase(wq_v, cache_v):
        def load_wq(p):
            return pltpu.make_async_copy(
                wq_ref.at[:, pl.ds(pl.multiple_of(p * width, 128), width)],
                wq_v.at[p], wq_sem.at[p],
            )

        load_cache = pltpu.make_async_copy(cache_ref, cache_v, local_sem.at[0])
        load_cache.start()
        loop(0, pairs, lambda p: load_wq(p).start())
        greet(n, me)
        loop(1, chips, lambda r: cq_copy(chips - r).start())
        cq_all[me] = cq_ref[...]
        cq_forward(me).start()
        load_cache.wait()

        def stage(r):
            t = chip ^ (chips - r)
            block = cache_v[request_ref[t * 2 * cand]]
            out_ref[t, 0] = block[:, :half_keys]
            out_ref[t, 1] = block[:, half_keys:]

        def stage_send(r):
            stage(r)
            send_blocks(r)

        loop(1, early, stage_send)
        loop(early, chips + 1, stage)
        k_in[me] = out_ref[chip]

        def relay_cq(r):
            s = me ^ (2 * (chips - r))
            remote(cq_ref, cq_all.at[s], cq_send.at[0], cq_recv.at[s], s).wait_recv()
            cq_forward(s).start()

        def wait_cq(r):
            s = me ^ (2 * (chips - r)) ^ 1
            remote(cq_all.at[s], cq_all.at[s], c_send.at[s], c_recv.at[s], sibling).wait_recv()

        loop(1, chips, relay_cq)
        loop(1, chips + 1, wait_cq)
        gathered = cq_all[...].astype(F32)
        x = jnp.concatenate(
            [gathered[:, :rows].reshape(n * rows, -1), gathered[:, rows:].reshape(n * rows, -1)],
            axis=1,
        ).astype(BF16)

        def project(p):
            load_wq(p).wait()
            y = jnp.dot(x, wq_v[p], preferred_element_type=F32)
            first = y[:, :kv].reshape(n, rows, kv)
            second = y[:, kv:].reshape(n, rows, kv)
            qs[:, pl.ds(pl.multiple_of(p * 2 * rows, 16), 2 * rows), :] = jnp.concatenate(
                [first, second], axis=1
            ).astype(BF16)

        loop(0, pairs, project)

    with jax.named_scope("start"):
        pl.run_scoped(
            start_phase,
            pltpu.VMEM((pairs, wq_ref.shape[0], width), BF16),
            pltpu.VMEM(cache_ref.shape, BF16),
        )

    def q_copy(j):
        return remote(qs.at[me ^ j], q_in.at[me], q_send.at[j], q_recv.at[me], me ^ j)

    loop(1, n, lambda r: q_copy(n - r).start())
    sibling_copy.start()
    loop(early, chips, send_blocks)
    q_in[me] = qs[me]

    row = lax.rem(lax.broadcasted_iota(jnp.int32, (block, 128), 0), rows)
    col = lax.broadcasted_iota(jnp.int32, (block, 128), 1)
    behind = row - col
    seen = (behind >= 0) & (behind <= lax.rem(row, steps))
    own_bias = jnp.where(seen, 0.0, -jnp.inf).astype(F32)

    def wait_q(r):
        s = me ^ (n - r)
        remote(qs.at[me], q_in.at[s], q_send.at[n - r], q_recv.at[s], s).wait_recv()

    with jax.named_scope("wait_queries"):
        loop(1, n, wait_q)

    def queries(b):
        return q_in[pl.ds(b * group, group)].reshape(block, kv)

    def own_terms(b):
        s = (
            lax.dot_general(queries(b), own_key_ref[...], nt, preferred_element_type=F32)
            * SCORE_SCALE
            + own_bias
        )
        own_score[b] = s
        top = jnp.maximum(s, -1e30)
        top_ref[b] = top
        sum_ref[b] = jnp.exp(s - top)

    loop(0, blocks, own_terms)

    request = request_ref[chip * 2 * cand]
    prompt = length_ref[request]
    owner = owner_ref[request]

    def pair_keys_of(t, features):
        return jnp.concatenate(
            [k_in[2 * t + i, h, :features, :] for i in (0, 1) for h in (0, 1)], axis=1
        )

    def pair_scores(score, t):
        keys = pair_keys_of(t, kv)
        at = lax.broadcasted_iota(jnp.int32, (1, pair_keys), 1)
        odd = (at >= segment).astype(jnp.int32)
        order = t * 2 + odd - owner
        order = jnp.where(order < 0, order + n, order)
        live = jnp.where(order * segment + at - odd * segment < prompt, 0.0, -jnp.inf).astype(F32)
        if v_in is not None:
            v_in[t] = keys[:latent].T

        def block_scores(b):
            s = (
                jnp.dot(queries(b), keys, preferred_element_type=F32) * SCORE_SCALE
                + live
            )
            score[b, t] = s
            old = top_ref[b]
            top = old
            for i in range(0, pair_keys, 128):
                top = jnp.maximum(top, s[:, i : i + 128])
            acc = sum_ref[b] * jnp.exp(old - top)
            for i in range(0, pair_keys, 128):
                acc = acc + jnp.exp(s[:, i : i + 128] - top)
            top_ref[b] = top
            sum_ref[b] = acc

        loop(0, blocks, block_scores)

    def forward_copy(s):
        return remote(k_in.at[s, core], k_in.at[s, core], f_send.at[s], f_recv.at[s], sibling)

    def relay(t):
        for other in (0, 1):
            s = t * 2 + other
            remote(
                out_ref.at[0, 0], k_in.at[s, core], k_send.at[0, 0], k_recv.at[s], s
            ).wait_recv()
            forward_copy(s).start()

    def arrive(t):
        for other in (0, 1):
            s = t * 2 + other
            remote(
                k_in.at[s, 1 - core], k_in.at[s, 1 - core], f_send.at[s], f_recv.at[s], sibling
            ).wait_recv()

    def lat_copy(d):
        return remote(lat_out.at[d], lat_ref.at[me], l_send.at[d], l_recv.at[me], d)

    def own_copy():
        return pltpu.make_async_copy(lat_out.at[me], lat_ref.at[me], local_sem.at[1])

    def each_block(score, r):
        b = (me // group) ^ (blocks - 1 - r)
        lane_top = top_ref[b]
        top = jnp.max(lane_top, axis=1, keepdims=True)
        inverse = 1.0 / jnp.sum(sum_ref[b] * jnp.exp(lane_top - top), axis=1, keepdims=True)
        total[...] = jnp.dot(
            (jnp.exp(own_score[b] - top) * inverse).astype(BF16), own_key_ref[:, :latent],
            preferred_element_type=F32,
        )

        def gather(t):
            weights = (jnp.exp(score[b, t] - top) * inverse).astype(BF16)
            if v_in is not None:
                total[...] += jnp.dot(weights, v_in[t], preferred_element_type=F32)
            else:
                total[...] += lax.dot_general(
                    weights, pair_keys_of(t, latent), nt, preferred_element_type=F32
                )

        loop(0, chips, gather)
        first = b * group
        lat_out[pl.ds(first, group)] = total[...].astype(BF16).reshape(group, per_source, latent)

        def send(i):
            d = first + i

            @pl.when(d != me)
            def _():
                lat_copy(d).start()

            @pl.when(d == me)
            def _():
                own_copy().start()

        loop(0, group, send)

    def main_phase(score):
        with jax.named_scope("own_scores"):
            loop(0, blocks, own_terms)
        relay(chip ^ (chips - 1))

        def receive(r):
            relay(chip ^ (chips - r))
            t = chip ^ (chips - r + 1)
            arrive(t)
            pair_scores(score, t)

        with jax.named_scope("receive"):
            loop(2, chips, receive)
            remote(
                out_ref.at[chip], k_in.at[sibling], k_send.at[0, 0], k_recv.at[sibling], sibling
            ).wait_recv()
            pair_scores(score, chip)
            arrive(chip ^ 1)
            pair_scores(score, chip ^ 1)
        with jax.named_scope("weighted_sums"):
            loop(0, blocks, lambda r: each_block(score, r))

    pl.run_scoped(main_phase, pltpu.VMEM((blocks, chips, block, pair_keys), F32))

    def finish(j):
        s = me ^ j
        q_copy(j).wait_send()
        remote(lat_out.at[me], lat_ref.at[s], l_send.at[s], l_recv.at[s], s).wait_recv()
        lat_copy(s).wait_send()

    def finish_blocks(j):
        cq_copy(j).wait_send()
        for half in (0, 1):
            block_copy(j, half).wait_send()
            forward_copy((chip ^ j) * 2 + half).wait_send()

    with jax.named_scope("wait_latents"):
        sibling_copy.wait_send()
        loop(1, chips, finish_blocks)
        loop(1, n, finish)
        loop(0, chips, lambda t: cq_forward(t * 2 + core).wait_send())
        own_copy().wait()


def lean_kernel(*args):
    at = 4 + 8 + 5
    attend_kernel(*args[:at], None, *args[at:])


def output_kernel(
    n, lat_ref, up_ref, wo_ref, o_ref,
    hv, wo_v, part, x_in, kept, y_out, y_in, snd, rcv,
    wo_sem, x_send, x_recv, y_send, y_recv, s_send, s_recv,
):
    me = lax.axis_index("xfer")
    chips = n // 2
    chip = me // 2
    core = lax.rem(me, 2)
    sibling = me ^ 1
    lines = chips // 2
    line = chip // 2
    side_of_pair = lax.rem(chip, 2)
    chunks = wo_v.shape[0]
    cw = wo_v.shape[3]
    half = chunks * cw
    heads, latent, value = up_ref.shape
    rows = lat_ref.shape[1] // heads

    def load_wo(j, side):
        return pltpu.make_async_copy(
            wo_ref.at[:, pl.ds(pl.multiple_of(j * cw + side * half, 128), cw)],
            wo_v.at[j, side], wo_sem.at[j, side],
        )

    def load(j):
        load_wo(j, 0).start()
        load_wo(j, 1).start()

    loop(0, chunks, load)
    greet(n, me)
    for p in range(heads // 2):
        z = lat_ref[:, p * 2 * rows : (p + 1) * 2 * rows, :].astype(F32)
        for i in (0, 1):
            h = 2 * p + i
            z_head = z[:, i * rows : (i + 1) * rows, :].reshape(n * rows, latent).astype(BF16)
            y = jnp.dot(z_head, up_ref[h], preferred_element_type=F32)
            y = y.reshape(chips, 2, rows, value)
            hv[0 : chips * rows, h * value : (h + 1) * value] = (
                y[:, 0].reshape(chips * rows, value).astype(BF16)
            )
            hv[chips * rows :, h * value : (h + 1) * value] = (
                y[:, 1].reshape(chips * rows, value).astype(BF16)
            )

    def core_copy(j):
        return remote(part.at[j, 1 - core], x_in.at[j], x_send.at[j], x_recv.at[j], sibling)

    def multiply(j):
        for side in (0, 1):
            load_wo(j, side).wait()
            y = jnp.dot(hv[...], wo_v[j, side], preferred_element_type=F32)
            part[j, 0, side] = y[: chips * rows]
            part[j, 1, side] = y[chips * rows :]
        core_copy(j).start()

    def pair_copy(j):
        return remote(y_out.at[j], y_in.at[j], y_send.at[j], y_recv.at[j], me ^ 2)

    def combine(j):
        core_copy(j).wait_recv()
        both = part[j, core] + x_in[j]
        packed = jnp.concatenate(
            [both[0].reshape(chips, rows, cw), both[1].reshape(chips, rows, cw)], axis=1
        ).reshape(lines, 2, 2 * rows, cw)
        kept[j] = jnp.where(side_of_pair == 0, packed[:, 0], packed[:, 1])
        y_out[j] = jnp.where(side_of_pair == 0, packed[:, 1], packed[:, 0]).astype(BF16)
        pair_copy(j).start()

    def line_copy(j, i):
        t = line ^ i
        return remote(
            snd.at[j, t], rcv.at[j, line], s_send.at[j, i], s_recv.at[j, line], me ^ (4 * i)
        )

    def spread(j):
        pair_copy(j).wait_recv()
        both = kept[j] + y_in[j].astype(F32)
        kept[j] = both
        snd[j] = both.astype(BF16)
        loop(1, lines, lambda i: line_copy(j, lines - i).start())

    multiply(0)
    multiply(1)
    combine(0)

    def step(j):
        multiply(j)
        combine(j - 1)
        spread(j - 2)

    loop(2, chunks, step)
    combine(chunks - 1)
    spread(chunks - 2)
    spread(chunks - 1)

    def finish(j):
        y = kept[j, line]
        for i in range(1, lines):
            s = line ^ i
            remote(
                snd.at[j, 0], rcv.at[j, s], s_send.at[j, i], s_recv.at[j, s], me ^ (4 * i)
            ).wait_recv()
            line_copy(j, i).wait_send()
            y = y + rcv[j, s].astype(F32)
        core_copy(j).wait_send()
        pair_copy(j).wait_send()
        o_ref[:, pl.ds(pl.multiple_of(j * cw, 128), cw)] = y[:rows].astype(BF16)
        o_ref[:, pl.ds(pl.multiple_of(half + j * cw, 128), cw)] = y[rows:].astype(BF16)

    loop(0, chunks, finish)


def params(collective_id, mib):
    return pltpu.CompilerParams(
        collective_id=collective_id, has_side_effects=True, vmem_limit_bytes=mib * MIB
    )


def shards(cq, new_kv, cache, prompt_len, prefill_owner, cand_req, w_q, value_up_weight, w_o):
    n = lax.axis_size("xfer")
    cand, steps, q_width = cq.shape
    heads, latent, value = value_up_weight.shape
    segment, kv = cache.shape[1:]
    rows = cand * steps
    model = w_o.shape[1]
    per_source = heads * rows
    chips = n // 2
    dma = pltpu.SemaphoreType.DMA

    smem = pl.BlockSpec(memory_space=pltpu.SMEM)
    cq_rows = cq.reshape(rows, q_width)
    cq_halves = jnp.concatenate([cq_rows[:, : q_width // 2], cq_rows[:, q_width // 2 :]], axis=0)
    own_keys = jnp.pad(new_kv.reshape(rows, kv), ((0, 128 - rows), (0, 0)))
    pairs = heads // 2
    keep = n <= 16
    block = 256
    blocks = n * per_source // block
    latents = pl.pallas_call(
        functools.partial(attend_kernel if keep else lean_kernel, n, cand, steps, chips // 4 + 1),
        out_shape=jax.ShapeDtypeStruct((n, per_source, latent), BF16),
        in_specs=[smem, smem, smem, VMEM, ANY, ANY, VMEM],
        out_specs=ANY,
        scratch_shapes=[
            pltpu.VMEM((n, 2 * rows, q_width // 2), BF16),
            pltpu.VMEM((n, per_source, kv), BF16),
            pltpu.VMEM((n, per_source, kv), BF16),
            pltpu.VMEM((chips, 2, kv, segment // 2), BF16),
            pltpu.VMEM((n, 2, kv, segment // 2), BF16),
            *([pltpu.VMEM((chips, 2 * segment, latent), BF16)] if keep else []),
            pltpu.VMEM((n, per_source, latent), BF16),
            pltpu.VMEM((blocks, block, 128), F32),
            pltpu.VMEM((blocks, block, 128), F32),
            pltpu.VMEM((blocks, block, 128), F32),
            pltpu.VMEM((block, latent), F32),
            dma((pairs,)),
            dma((n,)), dma((n,)), dma((n,)), dma((n,)),
            dma((chips, 2)), dma((n,)), dma((n,)), dma((n,)),
            dma((n,)), dma((n,)), dma((n,)), dma((n,)), dma((2,)),
        ],
        compiler_params=params(0, 60),
        name="attend",
    )(
        cand_req, prompt_len, prefill_owner, cq_halves, w_q,
        jnp.swapaxes(cache, 1, 2), own_keys,
    )

    cw = 512
    chunks = model // (2 * cw)
    out = pl.pallas_call(
        functools.partial(output_kernel, n),
        out_shape=jax.ShapeDtypeStruct((rows, model), BF16),
        in_specs=[VMEM, VMEM, ANY],
        out_specs=VMEM,
        scratch_shapes=[
            pltpu.VMEM((n * rows, heads * value), BF16),
            pltpu.VMEM((chunks, 2, heads * value, cw), BF16),
            pltpu.VMEM((chunks, 2, 2, chips * rows, cw), F32),
            pltpu.VMEM((chunks, 2, chips * rows, cw), F32),
            pltpu.VMEM((chunks, chips // 2, 2 * rows, cw), F32),
            *([pltpu.VMEM((chunks, chips // 2, 2 * rows, cw), BF16)] * 4),
            dma((chunks, 2)), dma((chunks,)), dma((chunks,)), dma((chunks,)), dma((chunks,)),
            dma((chunks, chips // 2)), dma((chunks, chips // 2)),
        ],
        compiler_params=params(1, 44),
        name="output",
    )(latents, value_up_weight, w_o)
    return out.reshape(cand, steps, model)


def solution(mesh):
    in_specs = (
        P(("grp", "xfer"), None, None),
        P(("grp", "xfer"), None, None),
        P("grp", "xfer", None),
        P("grp"),
        P("grp"),
        P("grp"),
        P(None, "xfer"),
        P("xfer", None, None),
        P("xfer", None),
    )
    out_specs = P(("grp", "xfer"), None, None)
    return jax.shard_map(shards, mesh=mesh, in_specs=in_specs, out_specs=out_specs, check_vma=False)
```

```python
import functools

import jax
import jax.numpy as jnp
from jax import lax
from jax.experimental import pallas as pl
from jax.experimental.pallas import tpu as pltpu
from jax.sharding import PartitionSpec as P

SCORE_SCALE = 0.135
BF16 = jnp.bfloat16
F32 = jnp.float32
ANY = pl.BlockSpec(memory_space=pl.ANY)
VMEM = pl.BlockSpec(memory_space=pltpu.VMEM)
MIB = 1 << 20


def greet(n, me):
    barrier = pltpu.get_barrier_semaphore()

    def hello(j, carry):
        pl.semaphore_signal(
            barrier, inc=1, device_id={"xfer": me ^ j},
            device_id_type=pl.DeviceIdType.MESH,
        )
        return carry

    lax.fori_loop(1, n, hello, 0)
    pl.semaphore_wait(barrier, n - 1)


def remote(src, dst, send, recv, device):
    return pltpu.make_async_remote_copy(
        src_ref=src, dst_ref=dst, send_sem=send, recv_sem=recv,
        device_id={"xfer": device}, device_id_type=pl.DeviceIdType.MESH,
    )


def loop(low, high, body):
    def step(i, carry):
        body(i)
        return carry

    lax.fori_loop(low, high, step, 0)


def hop(r, chips):
    odd = lax.rem(r, 2)
    return odd * (chips - 1) + (1 - odd) * (chips // 2) - lax.div(r, 2)


def attend_kernel(
    n, cand, steps, early, request_ref, length_ref, owner_ref, cq_ref, wq_ref, cache_ref,
    own_key_ref, lat_ref,
    cq_all, qs, q_in, out_ref, k_in, v_in, lat_out, own_score, top_ref, sum_ref, total,
    wq_sem, cq_send, cq_recv, q_send, q_recv, k_send, k_recv, f_send, f_recv,
    l_send, l_recv, c_send, c_recv, local_sem,
):
    me = lax.axis_index("xfer")
    chips = n // 2
    chip = me // 2
    core = lax.rem(me, 2)
    sibling = me ^ 1
    kv = q_in.shape[2]
    width = 2 * kv
    pairs = wq_ref.shape[1] // width
    rows = cq_ref.shape[0] // 2
    per_source, latent = lat_out.shape[1:]
    half_keys = k_in.shape[3]
    segment = 2 * half_keys
    pair_keys = 2 * segment
    block = total.shape[0]
    group = block // per_source
    blocks = n // group
    nt = (((1,), (1,)), ((), ()))

    def cq_copy(j):
        return remote(cq_ref, cq_all.at[me], cq_send.at[j], cq_recv.at[me], me ^ (2 * j))

    def cq_forward(s):
        return remote(cq_all.at[s], cq_all.at[s], c_send.at[s], c_recv.at[s], sibling)

    def block_copy(j, half):
        t = chip ^ j
        return remote(
            out_ref.at[t, half], k_in.at[me, half], k_send.at[j, half], k_recv.at[me], t * 2 + half
        )

    def send_blocks(r):
        block_copy(hop(r, chips), 0).start()
        block_copy(hop(r, chips), 1).start()

    sibling_copy = remote(
        out_ref.at[chip], k_in.at[me], k_send.at[0, 0], k_recv.at[me], sibling
    )

    def start_phase(wq_v, cache_v):
        def load_wq(p):
            return pltpu.make_async_copy(
                wq_ref.at[:, pl.ds(pl.multiple_of(p * width, 128), width)],
                wq_v.at[p], wq_sem.at[p],
            )

        load_cache = pltpu.make_async_copy(cache_ref, cache_v, local_sem.at[0])
        load_cache.start()
        loop(0, pairs, lambda p: load_wq(p).start())
        greet(n, me)
        loop(1, chips, lambda r: cq_copy(chips - r).start())
        cq_all[me] = cq_ref[...]
        cq_forward(me).start()
        load_cache.wait()

        def stage(r):
            t = chip ^ hop(r, chips)
            block = cache_v[request_ref[t * 2 * cand]]
            out_ref[t, 0] = block[:, :half_keys]
            out_ref[t, 1] = block[:, half_keys:]

        def stage_send(r):
            stage(r)
            send_blocks(r)

        loop(1, early, stage_send)
        loop(early, chips + 1, stage)
        k_in[me] = out_ref[chip]

        def relay_cq(r):
            s = me ^ (2 * (chips - r))
            remote(cq_ref, cq_all.at[s], cq_send.at[0], cq_recv.at[s], s).wait_recv()
            cq_forward(s).start()

        def wait_cq(r):
            s = me ^ (2 * (chips - r)) ^ 1
            remote(cq_all.at[s], cq_all.at[s], c_send.at[s], c_recv.at[s], sibling).wait_recv()

        loop(1, chips, relay_cq)
        loop(1, chips + 1, wait_cq)
        gathered = cq_all[...].astype(F32)
        x = jnp.concatenate(
            [gathered[:, :rows].reshape(n * rows, -1), gathered[:, rows:].reshape(n * rows, -1)],
            axis=1,
        ).astype(BF16)

        def project(p):
            load_wq(p).wait()
            y = jnp.dot(x, wq_v[p], preferred_element_type=F32)
            first = y[:, :kv].reshape(n, rows, kv)
            second = y[:, kv:].reshape(n, rows, kv)
            qs[:, pl.ds(pl.multiple_of(p * 2 * rows, 16), 2 * rows), :] = jnp.concatenate(
                [first, second], axis=1
            ).astype(BF16)

        loop(0, pairs, project)

    with jax.named_scope("start"):
        pl.run_scoped(
            start_phase,
            pltpu.VMEM((pairs, wq_ref.shape[0], width), BF16),
            pltpu.VMEM(cache_ref.shape, BF16),
        )

    def q_copy(j):
        return remote(qs.at[me ^ j], q_in.at[me], q_send.at[j], q_recv.at[me], me ^ j)

    loop(1, n, lambda r: q_copy(n - r).start())
    sibling_copy.start()
    loop(early, chips, send_blocks)
    q_in[me] = qs[me]

    row = lax.rem(lax.broadcasted_iota(jnp.int32, (block, 128), 0), rows)
    col = lax.broadcasted_iota(jnp.int32, (block, 128), 1)
    behind = row - col
    seen = (behind >= 0) & (behind <= lax.rem(row, steps))
    own_bias = jnp.where(seen, 0.0, -jnp.inf).astype(F32)

    def wait_q(r):
        s = me ^ (n - r)
        remote(qs.at[me], q_in.at[s], q_send.at[n - r], q_recv.at[s], s).wait_recv()

    with jax.named_scope("wait_queries"):
        loop(1, n, wait_q)

    def queries(b):
        return q_in[pl.ds(b * group, group)].reshape(block, kv)

    def own_terms(b):
        s = (
            lax.dot_general(queries(b), own_key_ref[...], nt, preferred_element_type=F32)
            * SCORE_SCALE
            + own_bias
        )
        own_score[b] = s
        top = jnp.maximum(s, -1e30)
        top_ref[b] = top
        sum_ref[b] = jnp.exp(s - top)

    loop(0, blocks, own_terms)

    request = request_ref[chip * 2 * cand]
    prompt = length_ref[request]
    owner = owner_ref[request]

    def pair_keys_of(t, features):
        return jnp.concatenate(
            [k_in[2 * t + i, h, :features, :] for i in (0, 1) for h in (0, 1)], axis=1
        )

    def pair_scores(score, t):
        keys = pair_keys_of(t, kv)
        at = lax.broadcasted_iota(jnp.int32, (1, pair_keys), 1)
        odd = (at >= segment).astype(jnp.int32)
        order = t * 2 + odd - owner
        order = jnp.where(order < 0, order + n, order)
        live = jnp.where(order * segment + at - odd * segment < prompt, 0.0, -jnp.inf).astype(F32)
        if v_in is not None:
            v_in[t] = keys[:latent].T

        def block_scores(b):
            s = (
                jnp.dot(queries(b), keys, preferred_element_type=F32) * SCORE_SCALE
                + live
            )
            score[b, t] = s
            old = top_ref[b]
            top = old
            for i in range(0, pair_keys, 128):
                top = jnp.maximum(top, s[:, i : i + 128])
            acc = sum_ref[b] * jnp.exp(old - top)
            for i in range(0, pair_keys, 128):
                acc = acc + jnp.exp(s[:, i : i + 128] - top)
            top_ref[b] = top
            sum_ref[b] = acc

        loop(0, blocks, block_scores)

    def forward_copy(s):
        return remote(k_in.at[s, core], k_in.at[s, core], f_send.at[s], f_recv.at[s], sibling)

    def relay(t):
        for other in (0, 1):
            s = t * 2 + other
            remote(
                out_ref.at[0, 0], k_in.at[s, core], k_send.at[0, 0], k_recv.at[s], s
            ).wait_recv()
            forward_copy(s).start()

    def arrive(t):
        for other in (0, 1):
            s = t * 2 + other
            remote(
                k_in.at[s, 1 - core], k_in.at[s, 1 - core], f_send.at[s], f_recv.at[s], sibling
            ).wait_recv()

    def lat_copy(d):
        return remote(lat_out.at[d], lat_ref.at[me], l_send.at[d], l_recv.at[me], d)

    def own_copy():
        return pltpu.make_async_copy(lat_out.at[me], lat_ref.at[me], local_sem.at[1])

    def each_block(score, r):
        b = (me // group) ^ (blocks - 1 - r)
        lane_top = top_ref[b]
        top = jnp.max(lane_top, axis=1, keepdims=True)
        inverse = 1.0 / jnp.sum(sum_ref[b] * jnp.exp(lane_top - top), axis=1, keepdims=True)
        total[...] = jnp.dot(
            (jnp.exp(own_score[b] - top) * inverse).astype(BF16), own_key_ref[:, :latent],
            preferred_element_type=F32,
        )

        def gather(t):
            weights = (jnp.exp(score[b, t] - top) * inverse).astype(BF16)
            if v_in is not None:
                total[...] += jnp.dot(weights, v_in[t], preferred_element_type=F32)
            else:
                total[...] += lax.dot_general(
                    weights, pair_keys_of(t, latent), nt, preferred_element_type=F32
                )

        loop(0, chips, gather)
        first = b * group
        lat_out[pl.ds(first, group)] = total[...].astype(BF16).reshape(group, per_source, latent)

        def send(i):
            d = first + i

            @pl.when(d != me)
            def _():
                lat_copy(d).start()

            @pl.when(d == me)
            def _():
                own_copy().start()

        loop(0, group, send)

    def main_phase(score):
        with jax.named_scope("own_scores"):
            loop(0, blocks, own_terms)
        relay(chip ^ (chips - 1))

        def receive(r):
            relay(chip ^ hop(r, chips))
            t = chip ^ hop(r - 1, chips)
            arrive(t)
            pair_scores(score, t)

        with jax.named_scope("receive"):
            remote(
                out_ref.at[chip], k_in.at[sibling], k_send.at[0, 0], k_recv.at[sibling], sibling
            ).wait_recv()
            pair_scores(score, chip)
            loop(2, chips, receive)
            arrive(chip ^ (chips // 2))
            pair_scores(score, chip ^ (chips // 2))
        with jax.named_scope("weighted_sums"):
            loop(0, blocks, lambda r: each_block(score, r))

    pl.run_scoped(main_phase, pltpu.VMEM((blocks, chips, block, pair_keys), F32))

    def finish(j):
        s = me ^ j
        q_copy(j).wait_send()
        remote(lat_out.at[me], lat_ref.at[s], l_send.at[s], l_recv.at[s], s).wait_recv()
        lat_copy(s).wait_send()

    def finish_blocks(j):
        cq_copy(j).wait_send()
        for half in (0, 1):
            block_copy(j, half).wait_send()
            forward_copy((chip ^ j) * 2 + half).wait_send()

    with jax.named_scope("wait_latents"):
        sibling_copy.wait_send()
        loop(1, chips, finish_blocks)
        loop(1, n, finish)
        loop(0, chips, lambda t: cq_forward(t * 2 + core).wait_send())
        own_copy().wait()


def lean_kernel(*args):
    at = 4 + 8 + 5
    attend_kernel(*args[:at], None, *args[at:])


def output_kernel(
    n, lat_ref, up_ref, wo_ref, o_ref,
    hv, wo_v, part, x_in, kept, y_out, y_in, snd, rcv,
    wo_sem, x_send, x_recv, y_send, y_recv, s_send, s_recv,
):
    me = lax.axis_index("xfer")
    chips = n // 2
    chip = me // 2
    core = lax.rem(me, 2)
    sibling = me ^ 1
    lines = chips // 2
    line = chip // 2
    side_of_pair = lax.rem(chip, 2)
    chunks = wo_v.shape[0]
    cw = wo_v.shape[3]
    half = chunks * cw
    heads, latent, value = up_ref.shape
    rows = lat_ref.shape[1] // heads

    def load_wo(j, side):
        return pltpu.make_async_copy(
            wo_ref.at[:, pl.ds(pl.multiple_of(j * cw + side * half, 128), cw)],
            wo_v.at[j, side], wo_sem.at[j, side],
        )

    def load(j):
        load_wo(j, 0).start()
        load_wo(j, 1).start()

    loop(0, chunks, load)
    greet(n, me)
    for p in range(heads // 2):
        z = lat_ref[:, p * 2 * rows : (p + 1) * 2 * rows, :].astype(F32)
        for i in (0, 1):
            h = 2 * p + i
            z_head = z[:, i * rows : (i + 1) * rows, :].reshape(n * rows, latent).astype(BF16)
            y = jnp.dot(z_head, up_ref[h], preferred_element_type=F32)
            y = y.reshape(chips, 2, rows, value)
            hv[0 : chips * rows, h * value : (h + 1) * value] = (
                y[:, 0].reshape(chips * rows, value).astype(BF16)
            )
            hv[chips * rows :, h * value : (h + 1) * value] = (
                y[:, 1].reshape(chips * rows, value).astype(BF16)
            )

    def core_copy(j):
        return remote(part.at[j, 1 - core], x_in.at[j], x_send.at[j], x_recv.at[j], sibling)

    def multiply(j):
        for side in (0, 1):
            load_wo(j, side).wait()
            y = jnp.dot(hv[...], wo_v[j, side], preferred_element_type=F32)
            part[j, 0, side] = y[: chips * rows]
            part[j, 1, side] = y[chips * rows :]
        core_copy(j).start()

    def pair_copy(j):
        return remote(y_out.at[j], y_in.at[j], y_send.at[j], y_recv.at[j], me ^ 2)

    def combine(j):
        core_copy(j).wait_recv()
        both = part[j, core] + x_in[j]
        packed = jnp.concatenate(
            [both[0].reshape(chips, rows, cw), both[1].reshape(chips, rows, cw)], axis=1
        ).reshape(lines, 2, 2 * rows, cw)
        kept[j] = jnp.where(side_of_pair == 0, packed[:, 0], packed[:, 1])
        y_out[j] = jnp.where(side_of_pair == 0, packed[:, 1], packed[:, 0]).astype(BF16)
        pair_copy(j).start()

    def line_copy(j, i):
        t = line ^ i
        return remote(
            snd.at[j, t], rcv.at[j, line], s_send.at[j, i], s_recv.at[j, line], me ^ (4 * i)
        )

    def spread(j):
        pair_copy(j).wait_recv()
        both = kept[j] + y_in[j].astype(F32)
        kept[j] = both
        snd[j] = both.astype(BF16)
        loop(1, lines, lambda i: line_copy(j, lines - i).start())

    for j in range(4):
        multiply(j)
    combine(0)
    combine(1)

    def step(j):
        multiply(j)
        combine(j - 2)
        spread(j - 4)

    loop(4, chunks, step)
    combine(chunks - 2)
    spread(chunks - 4)
    combine(chunks - 1)
    for j in range(chunks - 3, chunks):
        spread(j)

    def finish(j):
        y = kept[j, line]
        for i in range(1, lines):
            s = line ^ i
            remote(
                snd.at[j, 0], rcv.at[j, s], s_send.at[j, i], s_recv.at[j, s], me ^ (4 * i)
            ).wait_recv()
            line_copy(j, i).wait_send()
            y = y + rcv[j, s].astype(F32)
        core_copy(j).wait_send()
        pair_copy(j).wait_send()
        o_ref[:, pl.ds(pl.multiple_of(j * cw, 128), cw)] = y[:rows].astype(BF16)
        o_ref[:, pl.ds(pl.multiple_of(half + j * cw, 128), cw)] = y[rows:].astype(BF16)

    loop(0, chunks, finish)


def params(collective_id, mib):
    return pltpu.CompilerParams(
        collective_id=collective_id, has_side_effects=True, vmem_limit_bytes=mib * MIB
    )


def shards(cq, new_kv, cache, prompt_len, prefill_owner, cand_req, w_q, value_up_weight, w_o):
    n = lax.axis_size("xfer")
    cand, steps, q_width = cq.shape
    heads, latent, value = value_up_weight.shape
    segment, kv = cache.shape[1:]
    rows = cand * steps
    model = w_o.shape[1]
    per_source = heads * rows
    chips = n // 2
    dma = pltpu.SemaphoreType.DMA

    smem = pl.BlockSpec(memory_space=pltpu.SMEM)
    cq_rows = cq.reshape(rows, q_width)
    cq_halves = jnp.concatenate([cq_rows[:, : q_width // 2], cq_rows[:, q_width // 2 :]], axis=0)
    own_keys = jnp.pad(new_kv.reshape(rows, kv), ((0, 128 - rows), (0, 0)))
    pairs = heads // 2
    keep = n <= 16
    block = 256
    blocks = n * per_source // block
    latents = pl.pallas_call(
        functools.partial(attend_kernel if keep else lean_kernel, n, cand, steps, chips // 2 + 1),
        out_shape=jax.ShapeDtypeStruct((n, per_source, latent), BF16),
        in_specs=[smem, smem, smem, VMEM, ANY, ANY, VMEM],
        out_specs=ANY,
        scratch_shapes=[
            pltpu.VMEM((n, 2 * rows, q_width // 2), BF16),
            pltpu.VMEM((n, per_source, kv), BF16),
            pltpu.VMEM((n, per_source, kv), BF16),
            pltpu.VMEM((chips, 2, kv, segment // 2), BF16),
            pltpu.VMEM((n, 2, kv, segment // 2), BF16),
            *([pltpu.VMEM((chips, 2 * segment, latent), BF16)] if keep else []),
            pltpu.VMEM((n, per_source, latent), BF16),
            pltpu.VMEM((blocks, block, 128), F32),
            pltpu.VMEM((blocks, block, 128), F32),
            pltpu.VMEM((blocks, block, 128), F32),
            pltpu.VMEM((block, latent), F32),
            dma((pairs,)),
            dma((n,)), dma((n,)), dma((n,)), dma((n,)),
            dma((chips, 2)), dma((n,)), dma((n,)), dma((n,)),
            dma((n,)), dma((n,)), dma((n,)), dma((n,)), dma((2,)),
        ],
        compiler_params=params(0, 60),
        name="attend",
    )(
        cand_req, prompt_len, prefill_owner, cq_halves, w_q,
        jnp.swapaxes(cache, 1, 2), own_keys,
    )

    cw = 512
    chunks = model // (2 * cw)
    out = pl.pallas_call(
        functools.partial(output_kernel, n),
        out_shape=jax.ShapeDtypeStruct((rows, model), BF16),
        in_specs=[VMEM, VMEM, ANY],
        out_specs=VMEM,
        scratch_shapes=[
            pltpu.VMEM((n * rows, heads * value), BF16),
            pltpu.VMEM((chunks, 2, heads * value, cw), BF16),
            pltpu.VMEM((chunks, 2, 2, chips * rows, cw), F32),
            pltpu.VMEM((chunks, 2, chips * rows, cw), F32),
            pltpu.VMEM((chunks, chips // 2, 2 * rows, cw), F32),
            *([pltpu.VMEM((chunks, chips // 2, 2 * rows, cw), BF16)] * 4),
            dma((chunks, 2)), dma((chunks,)), dma((chunks,)), dma((chunks,)), dma((chunks,)),
            dma((chunks, chips // 2)), dma((chunks, chips // 2)),
        ],
        compiler_params=params(1, 44),
        name="output",
    )(latents, value_up_weight, w_o)
    return out.reshape(cand, steps, model)


def solution(mesh):
    in_specs = (
        P(("grp", "xfer"), None, None),
        P(("grp", "xfer"), None, None),
        P("grp", "xfer", None),
        P("grp"),
        P("grp"),
        P("grp"),
        P(None, "xfer"),
        P("xfer", None, None),
        P("xfer", None),
    )
    out_specs = P(("grp", "xfer"), None, None)
    return jax.shard_map(shards, mesh=mesh, in_specs=in_specs, out_specs=out_specs, check_vma=False)
```

```python
import functools

import jax
import jax.numpy as jnp
from jax import lax
from jax.experimental import pallas as pl
from jax.experimental.pallas import tpu as pltpu
from jax.sharding import PartitionSpec as P

SCORE_SCALE = 0.135
BF16 = jnp.bfloat16
F32 = jnp.float32
ANY = pl.BlockSpec(memory_space=pl.ANY)
VMEM = pl.BlockSpec(memory_space=pltpu.VMEM)
MIB = 1 << 20


def greet(n, me):
    barrier = pltpu.get_barrier_semaphore()

    def hello(j, carry):
        pl.semaphore_signal(
            barrier, inc=1, device_id={"xfer": me ^ j},
            device_id_type=pl.DeviceIdType.MESH,
        )
        return carry

    lax.fori_loop(1, n, hello, 0)
    pl.semaphore_wait(barrier, n - 1)


def remote(src, dst, send, recv, device):
    return pltpu.make_async_remote_copy(
        src_ref=src, dst_ref=dst, send_sem=send, recv_sem=recv,
        device_id={"xfer": device}, device_id_type=pl.DeviceIdType.MESH,
    )


def loop(low, high, body):
    def step(i, carry):
        body(i)
        return carry

    lax.fori_loop(low, high, step, 0)


def hop(r, chips):
    odd = lax.rem(r, 2)
    return odd * (chips - 1) + (1 - odd) * (chips // 2) - lax.div(r, 2)


def attend_kernel(
    n, cand, steps, early, request_ref, length_ref, owner_ref, cq_ref, wq_ref, cache_ref,
    own_key_ref, lat_ref,
    cq_all, qs, q_in, out_ref, k_in, v_in, lat_out, own_score, top_ref, sum_ref, total,
    wq_sem, cq_send, cq_recv, q_send, q_recv, k_send, k_recv, f_send, f_recv,
    l_send, l_recv, c_send, c_recv, local_sem,
):
    me = lax.axis_index("xfer")
    chips = n // 2
    chip = me // 2
    core = lax.rem(me, 2)
    sibling = me ^ 1
    kv = q_in.shape[2]
    width = 2 * kv
    pairs = wq_ref.shape[1] // width
    rows = cq_ref.shape[0] // 2
    per_source, latent = lat_out.shape[1:]
    half_keys = k_in.shape[3]
    segment = 2 * half_keys
    pair_keys = 2 * segment
    block = total.shape[0]
    group = block // per_source
    blocks = n // group
    nt = (((1,), (1,)), ((), ()))

    def cq_copy(j):
        return remote(cq_ref, cq_all.at[me], cq_send.at[j], cq_recv.at[me], me ^ (2 * j))

    def cq_forward(s):
        return remote(cq_all.at[s], cq_all.at[s], c_send.at[s], c_recv.at[s], sibling)

    def block_copy(j, half):
        t = chip ^ j
        return remote(
            out_ref.at[t, half], k_in.at[me, half], k_send.at[j, half], k_recv.at[me], t * 2 + half
        )

    def send_blocks(r):
        block_copy(hop(r, chips), 0).start()
        block_copy(hop(r, chips), 1).start()

    sibling_copy = remote(
        out_ref.at[chip], k_in.at[me], k_send.at[0, 0], k_recv.at[me], sibling
    )

    def start_phase(wq_v, cache_v):
        def load_wq(p):
            return pltpu.make_async_copy(
                wq_ref.at[:, pl.ds(pl.multiple_of(p * width, 128), width)],
                wq_v.at[p], wq_sem.at[p],
            )

        load_cache = pltpu.make_async_copy(cache_ref, cache_v, local_sem.at[0])
        load_cache.start()
        loop(0, pairs, lambda p: load_wq(p).start())
        greet(n, me)
        loop(1, chips, lambda r: cq_copy(chips - r).start())
        cq_all[me] = cq_ref[...]
        cq_forward(me).start()
        load_cache.wait()

        def stage(r):
            t = chip ^ hop(r, chips)
            block = cache_v[request_ref[t * 2 * cand]]
            out_ref[t, 0] = block[:, :half_keys]
            out_ref[t, 1] = block[:, half_keys:]

        def stage_send(r):
            stage(r)
            send_blocks(r)

        loop(1, early, stage_send)
        loop(early, chips + 1, stage)
        k_in[me] = out_ref[chip]

        def relay_cq(r):
            s = me ^ (2 * (chips - r))
            remote(cq_ref, cq_all.at[s], cq_send.at[0], cq_recv.at[s], s).wait_recv()
            cq_forward(s).start()

        def wait_cq(r):
            s = me ^ (2 * (chips - r)) ^ 1
            remote(cq_all.at[s], cq_all.at[s], c_send.at[s], c_recv.at[s], sibling).wait_recv()

        loop(1, chips, relay_cq)
        loop(1, chips + 1, wait_cq)
        gathered = cq_all[...].astype(F32)
        x = jnp.concatenate(
            [gathered[:, :rows].reshape(n * rows, -1), gathered[:, rows:].reshape(n * rows, -1)],
            axis=1,
        ).astype(BF16)

        def project(p):
            load_wq(p).wait()
            y = jnp.dot(x, wq_v[p], preferred_element_type=F32)
            first = y[:, :kv].reshape(n, rows, kv)
            second = y[:, kv:].reshape(n, rows, kv)
            qs[:, pl.ds(pl.multiple_of(p * 2 * rows, 16), 2 * rows), :] = jnp.concatenate(
                [first, second], axis=1
            ).astype(BF16)

        loop(0, pairs, project)

    with jax.named_scope("start"):
        pl.run_scoped(
            start_phase,
            pltpu.VMEM((pairs, wq_ref.shape[0], width), BF16),
            pltpu.VMEM(cache_ref.shape, BF16),
        )

    def q_copy(j):
        return remote(qs.at[me ^ j], q_in.at[me], q_send.at[j], q_recv.at[me], me ^ j)

    loop(1, n, lambda r: q_copy(n - r).start())
    sibling_copy.start()
    loop(early, chips, send_blocks)
    q_in[me] = qs[me]

    row = lax.rem(lax.broadcasted_iota(jnp.int32, (block, 128), 0), rows)
    col = lax.broadcasted_iota(jnp.int32, (block, 128), 1)
    behind = row - col
    seen = (behind >= 0) & (behind <= lax.rem(row, steps))
    own_bias = jnp.where(seen, 0.0, -jnp.inf).astype(F32)

    def wait_q(r):
        s = me ^ (n - r)
        remote(qs.at[me], q_in.at[s], q_send.at[n - r], q_recv.at[s], s).wait_recv()

    with jax.named_scope("wait_queries"):
        loop(1, n, wait_q)

    def queries(b):
        return q_in[pl.ds(b * group, group)].reshape(block, kv)

    def own_terms(b):
        s = (
            lax.dot_general(queries(b), own_key_ref[...], nt, preferred_element_type=F32)
            * SCORE_SCALE
            + own_bias
        )
        own_score[b] = s
        top = jnp.maximum(s, -1e30)
        top_ref[b] = top
        sum_ref[b] = jnp.exp(s - top)

    loop(0, blocks, own_terms)

    request = request_ref[chip * 2 * cand]
    prompt = length_ref[request]
    owner = owner_ref[request]

    def pair_keys_of(t, features):
        return jnp.concatenate(
            [k_in[2 * t + i, h, :features, :] for i in (0, 1) for h in (0, 1)], axis=1
        )

    def pair_scores(score, t):
        keys = pair_keys_of(t, kv)
        at = lax.broadcasted_iota(jnp.int32, (1, pair_keys), 1)
        odd = (at >= segment).astype(jnp.int32)
        order = t * 2 + odd - owner
        order = jnp.where(order < 0, order + n, order)
        live = jnp.where(order * segment + at - odd * segment < prompt, 0.0, -jnp.inf).astype(F32)
        if v_in is not None:
            v_in[t] = keys[:latent].T

        def block_scores(b):
            s = (
                jnp.dot(queries(b), keys, preferred_element_type=F32) * SCORE_SCALE
                + live
            )
            score[b, t] = s
            old = top_ref[b]
            top = old
            for i in range(0, pair_keys, 128):
                top = jnp.maximum(top, s[:, i : i + 128])
            acc = sum_ref[b] * jnp.exp(old - top)
            for i in range(0, pair_keys, 128):
                acc = acc + jnp.exp(s[:, i : i + 128] - top)
            top_ref[b] = top
            sum_ref[b] = acc

        loop(0, blocks, block_scores)

    def forward_copy(s):
        return remote(k_in.at[s, core], k_in.at[s, core], f_send.at[s], f_recv.at[s], sibling)

    def relay(t):
        for other in (0, 1):
            s = t * 2 + other
            remote(
                out_ref.at[0, 0], k_in.at[s, core], k_send.at[0, 0], k_recv.at[s], s
            ).wait_recv()
            forward_copy(s).start()

    def arrive(t):
        for other in (0, 1):
            s = t * 2 + other
            remote(
                k_in.at[s, 1 - core], k_in.at[s, 1 - core], f_send.at[s], f_recv.at[s], sibling
            ).wait_recv()

    def lat_copy(d):
        return remote(lat_out.at[d], lat_ref.at[me], l_send.at[d], l_recv.at[me], d)

    def own_copy():
        return pltpu.make_async_copy(lat_out.at[me], lat_ref.at[me], local_sem.at[1])

    def each_block(score, r):
        b = (me // group) ^ (blocks - 1 - r)
        lane_top = top_ref[b]
        top = jnp.max(lane_top, axis=1, keepdims=True)
        inverse = 1.0 / jnp.sum(sum_ref[b] * jnp.exp(lane_top - top), axis=1, keepdims=True)
        total[...] = jnp.dot(
            (jnp.exp(own_score[b] - top) * inverse).astype(BF16), own_key_ref[:, :latent],
            preferred_element_type=F32,
        )

        def gather(t):
            weights = (jnp.exp(score[b, t] - top) * inverse).astype(BF16)
            if v_in is not None:
                total[...] += jnp.dot(weights, v_in[t], preferred_element_type=F32)
            else:
                total[...] += lax.dot_general(
                    weights, pair_keys_of(t, latent), nt, preferred_element_type=F32
                )

        loop(0, chips, gather)
        first = b * group
        lat_out[pl.ds(first, group)] = total[...].astype(BF16).reshape(group, per_source, latent)

        def send(i):
            d = first + i

            @pl.when(d != me)
            def _():
                lat_copy(d).start()

            @pl.when(d == me)
            def _():
                own_copy().start()

        loop(0, group, send)

    def main_phase(score):
        with jax.named_scope("own_scores"):
            loop(0, blocks, own_terms)
        relay(chip ^ (chips - 1))

        def receive(r):
            relay(chip ^ hop(r, chips))
            t = chip ^ hop(r - 1, chips)
            arrive(t)
            pair_scores(score, t)

        with jax.named_scope("receive"):
            remote(
                out_ref.at[chip], k_in.at[sibling], k_send.at[0, 0], k_recv.at[sibling], sibling
            ).wait_recv()
            pair_scores(score, chip)
            loop(2, chips, receive)
            arrive(chip ^ (chips // 2))
            pair_scores(score, chip ^ (chips // 2))
        with jax.named_scope("weighted_sums"):
            loop(0, blocks, lambda r: each_block(score, r))

    pl.run_scoped(main_phase, pltpu.VMEM((blocks, chips, block, pair_keys), F32))

    def finish(j):
        s = me ^ j
        q_copy(j).wait_send()
        remote(lat_out.at[me], lat_ref.at[s], l_send.at[s], l_recv.at[s], s).wait_recv()
        lat_copy(s).wait_send()

    def finish_blocks(j):
        cq_copy(j).wait_send()
        for half in (0, 1):
            block_copy(j, half).wait_send()
            forward_copy((chip ^ j) * 2 + half).wait_send()

    with jax.named_scope("wait_latents"):
        sibling_copy.wait_send()
        loop(1, chips, finish_blocks)
        loop(1, n, finish)
        loop(0, chips, lambda t: cq_forward(t * 2 + core).wait_send())
        own_copy().wait()


def lean_kernel(*args):
    at = 4 + 8 + 5
    attend_kernel(*args[:at], None, *args[at:])


def output_kernel(
    n, lat_ref, up_ref, wo_ref, o_ref,
    hv, wo_v, part, x_in, kept, y_out, y_in, snd, rcv,
    wo_sem, x_send, x_recv, y_send, y_recv, s_send, s_recv,
):
    me = lax.axis_index("xfer")
    chips = n // 2
    chip = me // 2
    core = lax.rem(me, 2)
    sibling = me ^ 1
    lines = chips // 2
    line = chip // 2
    side_of_pair = lax.rem(chip, 2)
    chunks = wo_v.shape[0]
    cw = wo_v.shape[3]
    half = chunks * cw
    heads, latent, value = up_ref.shape
    rows = lat_ref.shape[1] // heads

    def load_wo(j, side):
        return pltpu.make_async_copy(
            wo_ref.at[:, pl.ds(pl.multiple_of(j * cw + side * half, 128), cw)],
            wo_v.at[j, side], wo_sem.at[j, side],
        )

    def load(j):
        load_wo(j, 0).start()
        load_wo(j, 1).start()

    loop(0, chunks, load)
    greet(n, me)
    for p in range(heads // 2):
        z = lat_ref[:, p * 2 * rows : (p + 1) * 2 * rows, :].astype(F32)
        for i in (0, 1):
            h = 2 * p + i
            z_head = z[:, i * rows : (i + 1) * rows, :].reshape(n * rows, latent).astype(BF16)
            y = jnp.dot(z_head, up_ref[h], preferred_element_type=F32)
            y = y.reshape(chips, 2, rows, value)
            hv[0 : chips * rows, h * value : (h + 1) * value] = (
                y[:, 0].reshape(chips * rows, value).astype(BF16)
            )
            hv[chips * rows :, h * value : (h + 1) * value] = (
                y[:, 1].reshape(chips * rows, value).astype(BF16)
            )

    def core_copy(j):
        return remote(part.at[j, 1 - core], x_in.at[j], x_send.at[j], x_recv.at[j], sibling)

    def multiply(j):
        for side in (0, 1):
            load_wo(j, side).wait()
            y = jnp.dot(hv[...], wo_v[j, side], preferred_element_type=F32)
            part[j, 0, side] = y[: chips * rows]
            part[j, 1, side] = y[chips * rows :]
        core_copy(j).start()

    def pair_copy(j):
        return remote(y_out.at[j], y_in.at[j], y_send.at[j], y_recv.at[j], me ^ 2)

    def combine(j):
        core_copy(j).wait_recv()
        both = part[j, core] + x_in[j]
        packed = jnp.concatenate(
            [both[0].reshape(chips, rows, cw), both[1].reshape(chips, rows, cw)], axis=1
        ).reshape(lines, 2, 2 * rows, cw)
        kept[j] = jnp.where(side_of_pair == 0, packed[:, 0], packed[:, 1])
        y_out[j] = jnp.where(side_of_pair == 0, packed[:, 1], packed[:, 0]).astype(BF16)
        pair_copy(j).start()

    def line_copy(j, i):
        t = line ^ i
        return remote(
            snd.at[j, t], rcv.at[j, line], s_send.at[j, i], s_recv.at[j, line], me ^ (4 * i)
        )

    def spread(j):
        pair_copy(j).wait_recv()
        both = kept[j] + y_in[j].astype(F32)
        kept[j] = both
        snd[j] = both.astype(BF16)
        loop(1, lines, lambda i: line_copy(j, lines - i).start())

    for j in range(4):
        multiply(j)
    combine(0)
    combine(1)

    def step(j):
        multiply(j)
        combine(j - 2)
        spread(j - 4)

    loop(4, chunks, step)
    combine(chunks - 2)
    spread(chunks - 4)
    combine(chunks - 1)
    for j in range(chunks - 3, chunks):
        spread(j)

    def finish(j):
        y = kept[j, line]
        for i in range(1, lines):
            s = line ^ i
            remote(
                snd.at[j, 0], rcv.at[j, s], s_send.at[j, i], s_recv.at[j, s], me ^ (4 * i)
            ).wait_recv()
            line_copy(j, i).wait_send()
            y = y + rcv[j, s].astype(F32)
        core_copy(j).wait_send()
        pair_copy(j).wait_send()
        o_ref[:, pl.ds(pl.multiple_of(j * cw, 128), cw)] = y[:rows].astype(BF16)
        o_ref[:, pl.ds(pl.multiple_of(half + j * cw, 128), cw)] = y[rows:].astype(BF16)

    loop(0, chunks, finish)


def params(collective_id, mib):
    return pltpu.CompilerParams(
        collective_id=collective_id, has_side_effects=True, vmem_limit_bytes=mib * MIB
    )


def shards(cq, new_kv, cache, prompt_len, prefill_owner, cand_req, w_q, value_up_weight, w_o):
    n = lax.axis_size("xfer")
    cand, steps, q_width = cq.shape
    heads, latent, value = value_up_weight.shape
    segment, kv = cache.shape[1:]
    rows = cand * steps
    model = w_o.shape[1]
    per_source = heads * rows
    chips = n // 2
    dma = pltpu.SemaphoreType.DMA

    smem = pl.BlockSpec(memory_space=pltpu.SMEM)
    cq_rows = cq.reshape(rows, q_width)
    cq_halves = jnp.concatenate([cq_rows[:, : q_width // 2], cq_rows[:, q_width // 2 :]], axis=0)
    own_keys = jnp.pad(new_kv.reshape(rows, kv), ((0, 128 - rows), (0, 0)))
    pairs = heads // 2
    keep = n <= 16
    block = 512
    blocks = n * per_source // block
    latents = pl.pallas_call(
        functools.partial(attend_kernel if keep else lean_kernel, n, cand, steps, chips // 2 + 1),
        out_shape=jax.ShapeDtypeStruct((n, per_source, latent), BF16),
        in_specs=[smem, smem, smem, VMEM, ANY, ANY, VMEM],
        out_specs=ANY,
        scratch_shapes=[
            pltpu.VMEM((n, 2 * rows, q_width // 2), BF16),
            pltpu.VMEM((n, per_source, kv), BF16),
            pltpu.VMEM((n, per_source, kv), BF16),
            pltpu.VMEM((chips, 2, kv, segment // 2), BF16),
            pltpu.VMEM((n, 2, kv, segment // 2), BF16),
            *([pltpu.VMEM((chips, 2 * segment, latent), BF16)] if keep else []),
            pltpu.VMEM((n, per_source, latent), BF16),
            pltpu.VMEM((blocks, block, 128), F32),
            pltpu.VMEM((blocks, block, 128), F32),
            pltpu.VMEM((blocks, block, 128), F32),
            pltpu.VMEM((block, latent), F32),
            dma((pairs,)),
            dma((n,)), dma((n,)), dma((n,)), dma((n,)),
            dma((chips, 2)), dma((n,)), dma((n,)), dma((n,)),
            dma((n,)), dma((n,)), dma((n,)), dma((n,)), dma((2,)),
        ],
        compiler_params=params(0, 60),
        name="attend",
    )(
        cand_req, prompt_len, prefill_owner, cq_halves, w_q,
        jnp.swapaxes(cache, 1, 2), own_keys,
    )

    cw = 512
    chunks = model // (2 * cw)
    out = pl.pallas_call(
        functools.partial(output_kernel, n),
        out_shape=jax.ShapeDtypeStruct((rows, model), BF16),
        in_specs=[VMEM, VMEM, ANY],
        out_specs=VMEM,
        scratch_shapes=[
            pltpu.VMEM((n * rows, heads * value), BF16),
            pltpu.VMEM((chunks, 2, heads * value, cw), BF16),
            pltpu.VMEM((chunks, 2, 2, chips * rows, cw), F32),
            pltpu.VMEM((chunks, 2, chips * rows, cw), F32),
            pltpu.VMEM((chunks, chips // 2, 2 * rows, cw), F32),
            *([pltpu.VMEM((chunks, chips // 2, 2 * rows, cw), BF16)] * 4),
            dma((chunks, 2)), dma((chunks,)), dma((chunks,)), dma((chunks,)), dma((chunks,)),
            dma((chunks, chips // 2)), dma((chunks, chips // 2)),
        ],
        compiler_params=params(1, 44),
        name="output",
    )(latents, value_up_weight, w_o)
    return out.reshape(cand, steps, model)


def solution(mesh):
    in_specs = (
        P(("grp", "xfer"), None, None),
        P(("grp", "xfer"), None, None),
        P("grp", "xfer", None),
        P("grp"),
        P("grp"),
        P("grp"),
        P(None, "xfer"),
        P("xfer", None, None),
        P("xfer", None),
    )
    out_specs = P(("grp", "xfer"), None, None)
    return jax.shard_map(shards, mesh=mesh, in_specs=in_specs, out_specs=out_specs, check_vma=False)
```
